1024 devices in a mesh: seq: 32 (over y, x_lo), fsdp: 32 (over z, x_hi, core).
Axes of the slice: x: 8 (x_hi: 2, x_lo: 4; x = x_hi * 4 + x_lo), y: 8, z: 8, core: 2. Of those that a mesh axis runs over, the one named last changes fastest.
Arguments:
- queries: bfloat16 [4096, 8192], P('seq', 'fsdp'), may hold values from -120 to 120
- keys: bfloat16 [4096, 1024], P('seq'), may hold values from -4 to 4
- values: bfloat16 [4096, 1024], P('seq'), may hold values from -6 to 6
- out_weight: bfloat16 [8192, 8192], P(None, 'fsdp'), may hold values from -0.09375 to 0.09375
- block_mask: int32 [64, 64], P(None, 'fsdp'), may hold values 0 or 1
Outputs:
- mixed: bfloat16 [4096, 8192], P('seq', 'fsdp')
The draws below stay inside these ranges and needn't reach their ends.
All inputs are finite; a program needn't handle non-finite values. No bound on the sum of `block_mask` on one device may be relied on, other than what follows from the above.
Results may differ from the reference program's by a relative error of at most 0.0085.
Values may be sent and summed in bfloat16 or wider, within the bound.
No kernel may reach another device: no remote copies, remote signals or barrier semaphores. Data moves between devices by JAX's collectives and lax.ppermute only.
A program may use at most 32 MiB of HBM per device.

```python
import math
import jax
import jax.numpy as jnp
from jax import lax

D = 8192
QH = 64
KVH = 8
HD = 128
BLOCK = 128
GROUP = 8
TOKENS = 4096


def shared_keys(key):
    base = jax.random.normal(key, (TOKENS, KVH * HD), jnp.float32)
    return jnp.clip(base, -4.0, 4.0)


def draw_keys(key, part):
    base = shared_keys(key)
    return base.astype(jnp.bfloat16)


def draw_queries(key, part):
    key = jax.random.fold_in(key, 7)
    fresh = jnp.clip(jax.random.normal(key, (TOKENS, QH * HD), jnp.float32), -4.0, 4.0)
    return fresh.astype(jnp.bfloat16)


def touch_ends(entries, own_key, smallest, top_value):
    index_at = [jax.random.randint(jax.random.fold_in(own_key, axis), (), 0, length) for axis, length in enumerate(entries.shape)]
    main_axis = entries.shape.index(max(entries.shape))
    beside = index_at[:main_axis] + [(index_at[main_axis] + 1) % entries.shape[main_axis]] + index_at[main_axis + 1:]
    return entries.at[tuple(index_at)].set(smallest).at[tuple(beside)].set(top_value)


def block_scale(own_key, shape, cuts, least, high):
    factor_of = 1.0
    for dim, blocks in cuts:
        heights = jax.random.uniform(jax.random.fold_in(jax.random.fold_in(own_key, 6), dim), (blocks,), jnp.float32, least / len(cuts), high / len(cuts))
        factor_of = factor_of * jnp.repeat(jnp.exp(heights), shape[dim] // blocks).reshape((-1,) + (1,) * (len(shape) - 1 - dim))
    return factor_of


def noise(own_key, extent, spread, most, pieces=(), held_as=jnp.bfloat16):
    entries = spread * jax.random.normal(own_key, extent, jnp.float32)
    if pieces:
        entries = entries * block_scale(own_key, extent, pieces, -0.22, 0.18)
    return jnp.clip(entries, -most, most).astype(held_as)


def setup_inputs(seed: int = 0) -> dict:
    key_list = jax.random.split(jax.random.key(seed), 6)
    queries = draw_queries(jax.random.fold_in(key_list[5], 71), 0)
    keys = draw_keys(jax.random.fold_in(key_list[5], 71), 0)
    values = noise(key_list[2], (TOKENS, KVH * HD), 1.0, 6.0, ((0, 32),))
    out_weight = noise(key_list[3], (QH * HD, D), (QH * HD // 2) ** -0.5, 0.09375, ((1, 32),))
    block_mask = touch_ends((jax.random.randint(key_list[4], (QH * HD // BLOCK, D // BLOCK), 0, 2) < 1).astype(jnp.int32), jax.random.fold_in(key_list[4], 1), 0, 1)
    return dict(queries=queries, keys=keys, values=values, out_weight=out_weight, block_mask=block_mask)


def one_head(query_head, key_head, value_head):
    scale = 1.0 / math.sqrt(HD)
    rows = math.gcd(TOKENS, 1024)
    blocks = query_head.reshape(TOKENS // rows, rows, HD)
    starts = jnp.arange(TOKENS // rows, dtype=jnp.int32) * rows
    key_pos = jnp.arange(TOKENS, dtype=jnp.int32)

    def one_block(item):
        block, start = item
        score = jnp.dot(block, key_head.T, preferred_element_type=jnp.float32) * scale
        query_pos = start + jnp.arange(rows, dtype=jnp.int32)
        allowed = query_pos[:, None] >= key_pos[None, :]
        score = jnp.where(allowed, score, jnp.float32(-1e+30))
        top = lax.optimization_barrier(jnp.max(score, axis=1, keepdims=True))
        expo = jnp.where(allowed, jnp.exp(score - top), jnp.float32(0.0))
        total = lax.optimization_barrier(jnp.sum(expo, axis=1, keepdims=True))
        summed = jnp.dot(expo.astype(jnp.bfloat16), value_head, preferred_element_type=jnp.float32)
        return (summed / total).astype(jnp.bfloat16)
    return lax.map(one_block, (blocks, starts)).reshape(TOKENS, HD)

def reference(queries, keys, values, out_weight, block_mask):
    query_heads = queries.reshape(TOKENS, QH, HD).transpose(1, 0, 2)
    key_heads = keys.reshape(TOKENS, KVH, HD).transpose(1, 0, 2)
    value_heads = values.reshape(TOKENS, KVH, HD).transpose(1, 0, 2)

    def per_head(index):
        shared = index // GROUP
        return one_head(query_heads[index], key_heads[shared], value_heads[shared])
    heads_out = lax.map(per_head, jnp.arange(QH, dtype=jnp.int32))
    heads_out = heads_out.transpose(1, 0, 2).reshape(TOKENS, QH * HD)
    keep = jnp.repeat(jnp.repeat(block_mask, BLOCK, axis=0), BLOCK, axis=1)
    pruned = out_weight * keep.astype(out_weight.dtype)
    return jnp.dot(heads_out, pruned, preferred_element_type=jnp.float32).astype(jnp.bfloat16)
```

```python
import math

import jax
import jax.numpy as jnp
from jax import lax
from jax.experimental import pallas as pl
from jax.experimental.pallas import tpu as pltpu
from jax.sharding import Mesh
from jax.sharding import PartitionSpec as P

HD = 128
BLOCK = 128
SIZES = (8, 4, 8, 2, 2)
AXES = ("y", "xl", "z", "xh", "core")
SEQ = ("y", "xl")
FSDP = ("z", "xh", "core")
N_SEQ = 32
N_CHIP = 16
CHUNK = 16
FACTOR = math.log2(math.e) / math.sqrt(HD)
LOWEST = -1e30
ANY = pl.BlockSpec(memory_space=pl.ANY)
VMEM = pl.BlockSpec(memory_space=pltpu.VMEM)
SMEM = pl.BlockSpec(memory_space=pltpu.SMEM)


def spread_kernel(keys_ref, values_ref, out_ref, piece, sems):
    half = piece.shape[0]
    column = pl.multiple_of(lax.axis_index("z") * HD, HD)
    row = pl.multiple_of(lax.axis_index("core") * half, half)
    place = (pl.ds(row, half), pl.ds(column, HD))
    key_copy = pltpu.make_async_copy(keys_ref.at[place], piece.at[:, :HD], sems.at[0])
    value_copy = pltpu.make_async_copy(values_ref.at[place], piece.at[:, HD:], sems.at[1])
    key_copy.start()
    value_copy.start()
    key_copy.wait()
    value_copy.wait()
    block = piece[...]
    for i in range(N_SEQ):
        out_ref[i] = block


def attend(queries_ref, kv_ref, from_core, top, total, summed):
    rows = queries_ref.shape[0]
    half = kv_ref.shape[1]
    width = CHUNK * half
    own = (lax.axis_index("y") * SIZES[1] + lax.axis_index("xl")) * rows
    q = jnp.concatenate([queries_ref[:, :HD], queries_ref[:, HD:]], axis=0)
    query_pos = own + lax.broadcasted_iota(jnp.int32, (2 * rows, width), 0) % rows
    column = lax.broadcasted_iota(jnp.int32, (2 * rows, width), 1)
    key_pos = column // half * rows + column % half + from_core * half
    ahead = query_pos - key_pos
    for first in range(0, N_SEQ, CHUNK):
        key = kv_ref[first : first + CHUNK, :, :HD].reshape(width, HD)
        value = kv_ref[first : first + CHUNK, :, HD:].reshape(width, HD)
        score = lax.dot_general(
            q, key, (((1,), (1,)), ((), ())), preferred_element_type=jnp.float32
        )
        score = jnp.where(ahead >= first * rows, score, jnp.float32(LOWEST))
        new_top = jnp.max(score, axis=1, keepdims=True)
        if top is not None:
            new_top = jnp.maximum(top, new_top)
        expo = jnp.exp2((score - new_top) * FACTOR)
        part = jnp.sum(expo, axis=1, keepdims=True)
        product = jnp.dot(expo.astype(jnp.bfloat16), value, preferred_element_type=jnp.float32)
        if top is None:
            total, summed = part, product
        else:
            fix = jnp.exp2((top - new_top) * FACTOR)
            total, summed = total * fix + part, summed * fix + product
        top = new_top
    return top, total, summed


def attention_own_kernel(queries_ref, kv_ref, top_ref, total_ref, summed_ref):
    top, total, summed = attend(queries_ref, kv_ref, lax.axis_index("core"), None, None, None)
    top_ref[...] = jnp.broadcast_to(top, top_ref.shape)
    total_ref[...] = jnp.broadcast_to(total, total_ref.shape)
    summed_ref[...] = summed


def attention_other_kernel(queries_ref, kv_ref, top_ref, total_ref, summed_ref, out_ref):
    rows = queries_ref.shape[0]
    _, total, summed = attend(
        queries_ref,
        kv_ref,
        1 - lax.axis_index("core"),
        top_ref[:, :1],
        total_ref[:, :1],
        summed_ref[...],
    )
    normed = (summed / total).astype(jnp.bfloat16)
    heads = jnp.concatenate([normed[:rows], normed[rows:]], axis=1)
    for i in range(N_CHIP):
        out_ref[i] = heads


def project(mask_ref, heads_ref, weight_ref, from_core):
    columns = weight_ref.shape[1]
    total = jnp.zeros((heads_ref.shape[1], columns), jnp.float32)
    for chip in range(N_CHIP):
        rows = []
        for i in range(2):
            block = (chip * 2 + from_core) * 2 + i
            at = pl.ds(pl.multiple_of(block * BLOCK, BLOCK), BLOCK)
            line = []
            for j in range(columns // BLOCK):
                keep = mask_ref[j, block].astype(jnp.float32).astype(jnp.bfloat16)
                line.append(weight_ref[at, j * BLOCK : (j + 1) * BLOCK] * keep)
            rows.append(jnp.concatenate(line, axis=1))
        pruned = jnp.concatenate(rows, axis=0)
        total += jnp.dot(heads_ref[chip], pruned, preferred_element_type=jnp.float32)
    return total


def project_own_kernel(mask_ref, heads_ref, weight_ref, out_ref):
    out_ref[...] = project(mask_ref, heads_ref, weight_ref, lax.axis_index("core"))


def project_other_kernel(mask_ref, heads_ref, weight_ref, part_ref, out_ref):
    rest = project(mask_ref, heads_ref, weight_ref, 1 - lax.axis_index("core"))
    out_ref[...] = (part_ref[...] + rest).astype(out_ref.dtype)


def per_device(queries, keys, values, out_weight, block_mask):
    rows = queries.shape[0]
    columns = out_weight.shape[1]
    half = rows // 2
    mask = block_mask.T
    params = pltpu.CompilerParams(vmem_limit_bytes=32 * 2**20)
    shape = jax.ShapeDtypeStruct
    spread = pl.pallas_call(
        spread_kernel,
        out_shape=shape((N_SEQ, half, 2 * HD), jnp.bfloat16),
        in_specs=[ANY, ANY],
        out_specs=VMEM,
        scratch_shapes=[pltpu.VMEM((half, 2 * HD), jnp.bfloat16), pltpu.SemaphoreType.DMA((2,))],
        name="spread_kv",
    )(keys, values)
    swap = [(0, 1), (1, 0)]
    own = lax.all_to_all(spread, SEQ, 0, 0, tiled=True)
    other = lax.ppermute(own, "core", swap)
    state = shape((2 * rows, HD), jnp.float32)
    carry = pl.pallas_call(
        attention_own_kernel,
        out_shape=[state] * 3,
        in_specs=[VMEM] * 2,
        out_specs=[VMEM] * 3,
        compiler_params=params,
        cost_estimate=pl.CostEstimate(flops=2**29, bytes_accessed=2**21, transcendentals=2**19),
        name="attention_own",
    )(queries, own)
    heads = pl.pallas_call(
        attention_other_kernel,
        out_shape=shape((N_CHIP, rows, 2 * HD), jnp.bfloat16),
        in_specs=[VMEM] * 5,
        out_specs=VMEM,
        compiler_params=params,
        cost_estimate=pl.CostEstimate(flops=2**29, bytes_accessed=2**21, transcendentals=2**19),
        name="attention_other",
    )(queries, other, *carry)
    own_heads = lax.all_to_all(heads, ("z", "xh"), 0, 0, tiled=True)
    other_heads = lax.ppermute(own_heads, "core", swap)
    part = pl.pallas_call(
        project_own_kernel,
        out_shape=shape((rows, columns), jnp.float32),
        in_specs=[SMEM, VMEM, VMEM],
        out_specs=VMEM,
        compiler_params=params,
        cost_estimate=pl.CostEstimate(flops=2**28, bytes_accessed=2**22, transcendentals=0),
        name="project_own",
    )(mask, own_heads, out_weight)
    return pl.pallas_call(
        project_other_kernel,
        out_shape=shape((rows, columns), jnp.bfloat16),
        in_specs=[SMEM, VMEM, VMEM, VMEM],
        out_specs=VMEM,
        compiler_params=params,
        cost_estimate=pl.CostEstimate(flops=2**28, bytes_accessed=2**22, transcendentals=0),
        name="project_other",
    )(mask, other_heads, out_weight, part)


def solution(mesh):
    fine = Mesh(mesh.devices.reshape(SIZES), AXES)
    return jax.shard_map(
        per_device,
        mesh=fine,
        in_specs=(P(SEQ, FSDP), P(SEQ, None), P(SEQ, None), P(None, FSDP), P(None, FSDP)),
        out_specs=P(SEQ, FSDP),
        check_vma=False,
    )
```

```python
import math

import jax
import jax.numpy as jnp
from jax import lax
from jax.experimental import pallas as pl
from jax.experimental.pallas import tpu as pltpu
from jax.sharding import Mesh
from jax.sharding import PartitionSpec as P

HD = 128
BLOCK = 128
SIZES = (8, 4, 8, 2, 2)
AXES = ("y", "xl", "z", "xh", "core")
SEQ = ("y", "xl")
FSDP = ("z", "xh", "core")
N_SEQ = 32
N_CHIP = 16
FACTOR = math.log2(math.e) / math.sqrt(HD)
LOWEST = -1e30
ANY = pl.BlockSpec(memory_space=pl.ANY)
VMEM = pl.BlockSpec(memory_space=pltpu.VMEM)
SMEM = pl.BlockSpec(memory_space=pltpu.SMEM)


def spread_kernel(queries_ref, keys_ref, values_ref, own_ref, out_ref, pieces, sems):
    rows = keys_ref.shape[0]
    part = pieces.shape[1]
    column = pl.multiple_of(lax.axis_index("z") * HD, HD)
    core = lax.axis_index("core")
    copies = [pltpu.make_async_copy(queries_ref, own_ref, sems.at[4])]
    for parity in range(2):
        row = pl.multiple_of(parity * (rows // 2) + core * part, part)
        place = (pl.ds(row, part), pl.ds(column, HD))
        for i, source in enumerate((keys_ref, values_ref)):
            target = pieces.at[parity, :, i * HD : (i + 1) * HD]
            copies.append(pltpu.make_async_copy(source.at[place], target, sems.at[parity * 2 + i]))
    for copy in copies:
        copy.start()
    for copy in copies:
        copy.wait()
    blocks = pieces[0], pieces[1]
    for i in range(N_SEQ):
        out_ref[i] = blocks[i % 2]


def attend(queries_ref, kv_ref, of_partner, from_core, state):
    rows = queries_ref.shape[0]
    part = kv_ref.shape[1]
    width = N_SEQ * part
    xl = lax.axis_index("xl")
    parity = lax.rem(xl, 2)
    start = (lax.axis_index("y") * SIZES[1] + xl) * rows
    if of_partner:
        start = start + (1 - 2 * parity) * rows
    q = jnp.concatenate([queries_ref[:, :HD], queries_ref[:, HD:]], axis=0)
    query_pos = start + lax.broadcasted_iota(jnp.int32, (2 * rows, 1), 0) % rows
    column = lax.broadcasted_iota(jnp.int32, (1, width), 1)
    key_pos = column // part * rows + column % part + (parity * 2 + from_core) * part
    key = kv_ref[:, :, :HD].reshape(width, HD)
    value = kv_ref[:, :, HD:].reshape(width, HD)
    score = lax.dot_general(q, key, (((1,), (1,)), ((), ())), preferred_element_type=jnp.float32)
    score = jnp.where(query_pos >= key_pos, score, jnp.float32(LOWEST))
    new_top = jnp.max(score, axis=1, keepdims=True)
    if state is not None:
        new_top = jnp.maximum(state[0], new_top)
    expo = jnp.exp2((score - new_top) * FACTOR)
    total = jnp.sum(expo, axis=1, keepdims=True)
    summed = jnp.dot(expo.astype(jnp.bfloat16), value, preferred_element_type=jnp.float32)
    if state is not None:
        fix = jnp.exp2((state[0] - new_top) * FACTOR)
        total = total + state[1] * fix
        summed = summed + state[2] * fix
    return new_top, total, summed


def attention_own_kernel(queries_ref, kv_ref, top_ref, total_ref, summed_ref):
    state = attend(queries_ref, kv_ref, False, lax.axis_index("core"), None)
    for ref, value in zip((top_ref, total_ref, summed_ref), state):
        ref[...] = jnp.broadcast_to(value, ref.shape)


def bf16_pieces(value):
    pieces = []
    for _ in range(3):
        piece = value.astype(jnp.bfloat16)
        pieces.append(piece)
        value = value - piece.astype(jnp.float32)
    return pieces


def attention_other_kernel(
    queries_ref, partner_ref, own_ref, other_ref, top_in, total_in, summed_in,
    top_ref, total_ref, summed_ref, sent_ref,
):
    rows = queries_ref.shape[0]
    core = lax.axis_index("core")
    state = top_in[:, :1], total_in[:, :1], summed_in[...]
    state = attend(queries_ref, other_ref, False, 1 - core, state)
    for ref, value in zip((top_ref, total_ref, summed_ref), state):
        ref[...] = jnp.broadcast_to(value, ref.shape)
    state = attend(partner_ref, own_ref, True, core, None)
    top, total, summed = attend(partner_ref, other_ref, True, 1 - core, state)
    lane = lax.broadcasted_iota(jnp.int32, (rows, HD), 1)
    notes = jnp.zeros((rows, HD), jnp.float32)
    for head in range(2):
        at = slice(head * rows, (head + 1) * rows)
        sent_ref[:, head * HD : (head + 1) * HD] = summed[at].astype(jnp.bfloat16)
        pieces = bf16_pieces(top[at]) + bf16_pieces(total[at])
        for i, piece in enumerate(pieces):
            notes = jnp.where(lane == head * 8 + i, piece.astype(jnp.float32), notes)
    sent_ref[:, 2 * HD :] = notes.astype(jnp.bfloat16)


def merge_kernel(top_ref, total_ref, summed_ref, got_ref, out_ref):
    rows = got_ref.shape[0]
    notes = got_ref[:, 2 * HD :].astype(jnp.float32)
    heads = []
    for head in range(2):
        at = slice(head * rows, (head + 1) * rows)
        own_top, own_total = top_ref[at, :1], total_ref[at, :1]
        first = head * 8
        top = notes[:, first : first + 1] + notes[:, first + 1 : first + 2] + notes[:, first + 2 : first + 3]
        total = notes[:, first + 3 : first + 4] + notes[:, first + 4 : first + 5] + notes[:, first + 5 : first + 6]
        new_top = jnp.maximum(own_top, top)
        own_fix = jnp.exp2((own_top - new_top) * FACTOR)
        fix = jnp.exp2((top - new_top) * FACTOR)
        summed = got_ref[:, head * HD : (head + 1) * HD].astype(jnp.float32)
        summed = summed_ref[at] * own_fix + summed * fix
        heads.append((summed / (own_total * own_fix + total * fix)).astype(jnp.bfloat16))
    block = jnp.concatenate(heads, axis=1)
    for i in range(N_CHIP):
        out_ref[i] = block


def project(mask_ref, heads_ref, weight_ref, from_core):
    columns = weight_ref.shape[1]
    total = jnp.zeros((heads_ref.shape[1], columns), jnp.float32)
    for chip in range(N_CHIP):
        rows = []
        for i in range(2):
            block = (chip * 2 + from_core) * 2 + i
            at = pl.ds(pl.multiple_of(block * BLOCK, BLOCK), BLOCK)
            line = []
            for j in range(columns // BLOCK):
                keep = mask_ref[j, block].astype(jnp.float32).astype(jnp.bfloat16)
                line.append(weight_ref[at, j * BLOCK : (j + 1) * BLOCK] * keep)
            rows.append(jnp.concatenate(line, axis=1))
        pruned = jnp.concatenate(rows, axis=0)
        total += jnp.dot(heads_ref[chip], pruned, preferred_element_type=jnp.float32)
    return total


def project_own_kernel(mask_ref, heads_ref, weight_ref, out_ref):
    out_ref[...] = project(mask_ref, heads_ref, weight_ref, lax.axis_index("core"))


def project_other_kernel(mask_ref, heads_ref, weight_ref, part_ref, out_ref):
    rest = project(mask_ref, heads_ref, weight_ref, 1 - lax.axis_index("core"))
    out_ref[...] = (part_ref[...] + rest).astype(out_ref.dtype)


def per_device(queries, keys, values, out_weight, block_mask):
    rows = queries.shape[0]
    columns = out_weight.shape[1]
    part = rows // 4
    mask = block_mask.T
    params = pltpu.CompilerParams(vmem_limit_bytes=32 * 2**20)
    shape = jax.ShapeDtypeStruct
    cost = pl.CostEstimate(flops=2**29, bytes_accessed=2**21, transcendentals=2**19)
    own_queries, spread = pl.pallas_call(
        spread_kernel,
        out_shape=[
            shape((rows, 2 * HD), jnp.bfloat16),
            shape((N_SEQ, part, 2 * HD), jnp.bfloat16),
        ],
        in_specs=[ANY] * 3,
        out_specs=[VMEM] * 2,
        scratch_shapes=[
            pltpu.VMEM((2, part, 2 * HD), jnp.bfloat16),
            pltpu.SemaphoreType.DMA((5,)),
        ],
        name="spread_kv",
    )(queries, keys, values)
    swap = [(0, 1), (1, 0)]
    swap_x = [(0, 1), (1, 0), (2, 3), (3, 2)]
    partner_queries = lax.ppermute(queries, "xl", swap_x)
    spread, partner_queries = lax.optimization_barrier((spread, partner_queries))
    own = lax.all_to_all(spread, SEQ, 0, 0, tiled=True)
    other = lax.ppermute(own, "core", swap)
    state = pl.pallas_call(
        attention_own_kernel,
        out_shape=[shape((2 * rows, HD), jnp.float32)] * 3,
        in_specs=[VMEM] * 2,
        out_specs=[VMEM] * 3,
        compiler_params=params,
        cost_estimate=cost,
        name="attention_own",
    )(own_queries, own)
    *state, sent = pl.pallas_call(
        attention_other_kernel,
        out_shape=[shape((2 * rows, HD), jnp.float32)] * 3 + [shape((rows, 3 * HD), jnp.bfloat16)],
        in_specs=[VMEM] * 7,
        out_specs=[VMEM] * 4,
        compiler_params=params,
        cost_estimate=cost,
        name="attention_other",
    )(own_queries, partner_queries, own, other, *state)
    got = lax.ppermute(sent, "xl", swap_x)
    heads = pl.pallas_call(
        merge_kernel,
        out_shape=shape((N_CHIP, rows, 2 * HD), jnp.bfloat16),
        in_specs=[VMEM] * 4,
        out_specs=VMEM,
        compiler_params=params,
        name="merge",
    )(*state, got)
    own_heads = lax.all_to_all(heads, ("z", "xh"), 0, 0, tiled=True)
    other_heads = lax.ppermute(own_heads, "core", swap)
    part = pl.pallas_call(
        project_own_kernel,
        out_shape=shape((rows, columns), jnp.float32),
        in_specs=[SMEM, VMEM, VMEM],
        out_specs=VMEM,
        compiler_params=params,
        cost_estimate=pl.CostEstimate(flops=2**28, bytes_accessed=2**22, transcendentals=0),
        name="project_own",
    )(mask, own_heads, out_weight)
    return pl.pallas_call(
        project_other_kernel,
        out_shape=shape((rows, columns), jnp.bfloat16),
        in_specs=[SMEM, VMEM, VMEM, VMEM],
        out_specs=VMEM,
        compiler_params=params,
        cost_estimate=pl.CostEstimate(flops=2**28, bytes_accessed=2**22, transcendentals=0),
        name="project_other",
    )(mask, other_heads, out_weight, part)


def solution(mesh):
    fine = Mesh(mesh.devices.reshape(SIZES), AXES)
    return jax.shard_map(
        per_device,
        mesh=fine,
        in_specs=(P(SEQ, FSDP), P(SEQ, None), P(SEQ, None), P(None, FSDP), P(None, FSDP)),
        out_specs=P(SEQ, FSDP),
        check_vma=False,
    )
```

```python
import math

import jax
import jax.numpy as jnp
from jax import lax
from jax.experimental import pallas as pl
from jax.experimental.pallas import tpu as pltpu
from jax.sharding import Mesh
from jax.sharding import PartitionSpec as P

HD = 128
BLOCK = 128
SIZES = (8, 4, 8, 2, 2)
AXES = ("y", "xl", "z", "xh", "core")
SEQ = ("y", "xl")
FSDP = ("z", "xh", "core")
N_SEQ = 32
N_Z = 8
FACTOR = math.log2(math.e) / math.sqrt(HD)
LOWEST = -1e30
ANY = pl.BlockSpec(memory_space=pl.ANY)
VMEM = pl.BlockSpec(memory_space=pltpu.VMEM)
SMEM = pl.BlockSpec(memory_space=pltpu.SMEM)


def spread_kernel(keys_ref, values_ref, out_ref, piece, sems):
    half = piece.shape[0]
    column = pl.multiple_of(lax.axis_index("z") * HD, HD)
    row = pl.multiple_of(lax.axis_index("core") * half, half)
    place = (pl.ds(row, half), pl.ds(column, HD))
    copies = [
        pltpu.make_async_copy(keys_ref.at[place], piece.at[:, :HD], sems.at[0]),
        pltpu.make_async_copy(values_ref.at[place], piece.at[:, HD:], sems.at[1]),
    ]
    for copy in copies:
        copy.start()
    for copy in copies:
        copy.wait()
    block = piece[...]
    for i in range(N_SEQ):
        out_ref[i] = block


def attend(queries_ref, kv_ref, from_core, state):
    rows = queries_ref.shape[0]
    half = kv_ref.shape[1]
    width = N_SEQ * half
    start = (lax.axis_index("y") * SIZES[1] + lax.axis_index("xl")) * rows
    q = jnp.concatenate([queries_ref[:, :HD], queries_ref[:, HD:]], axis=0)
    query_pos = start + lax.broadcasted_iota(jnp.int32, (2 * rows, 1), 0) % rows
    column = lax.broadcasted_iota(jnp.int32, (1, width), 1)
    key_pos = column // half * rows + column % half + from_core * half
    key = kv_ref[:, :, :HD].reshape(width, HD)
    value = kv_ref[:, :, HD:].reshape(width, HD)
    score = lax.dot_general(q, key, (((1,), (1,)), ((), ())), preferred_element_type=jnp.float32)
    score = jnp.where(query_pos >= key_pos, score, jnp.float32(LOWEST))
    top = jnp.max(score, axis=1, keepdims=True)
    if state is not None:
        top = jnp.maximum(state[0], top)
    expo = jnp.exp2((score - top) * FACTOR)
    total = jnp.sum(expo, axis=1, keepdims=True)
    summed = jnp.dot(expo.astype(jnp.bfloat16), value, preferred_element_type=jnp.float32)
    if state is not None:
        fix = jnp.exp2((state[0] - top) * FACTOR)
        total = total + state[1] * fix
        summed = summed + state[2] * fix
    return top, total, summed


def finish(state):
    _, total, summed = state
    rows = total.shape[0] // 2
    normed = (summed / total).astype(jnp.bfloat16)
    return jnp.concatenate([normed[:rows], normed[rows:]], axis=1)


def attention_first_kernel(queries_ref, kv_ref, top_ref, total_ref, summed_ref):
    state = attend(queries_ref, kv_ref, lax.axis_index("core"), None)
    for ref, value in zip((top_ref, total_ref, summed_ref), state):
        ref[...] = jnp.broadcast_to(value, ref.shape)


def attention_second_kernel(queries_ref, kv_ref, top_ref, total_ref, summed_ref, out_ref):
    state = top_ref[:, :1], total_ref[:, :1], summed_ref[...]
    out_ref[...] = finish(attend(queries_ref, kv_ref, 1 - lax.axis_index("core"), state))


def attention_partner_kernel(queries_ref, own_ref, other_ref, heads_ref, out_ref):
    core = lax.axis_index("core")
    state = attend(queries_ref, own_ref, core, None)
    partner = finish(attend(queries_ref, other_ref, 1 - core, state))
    heads = jnp.concatenate([heads_ref[...], partner], axis=1)
    for i in range(N_Z):
        out_ref[i] = heads


def project(mask_ref, heads_ref, weight_ref, from_core):
    columns = weight_ref.shape[1]
    total = jnp.zeros((heads_ref.shape[1], columns), jnp.float32)
    xh = lax.axis_index("xh")
    for z in range(N_Z):
        rows = []
        for chip in (z * 2 + xh, z * 2 + 1 - xh):
            for i in range(2):
                block = (chip * 2 + from_core) * 2 + i
                at = pl.ds(pl.multiple_of(block * BLOCK, BLOCK), BLOCK)
                line = []
                for j in range(columns // BLOCK):
                    keep = mask_ref[j, block].astype(jnp.float32).astype(jnp.bfloat16)
                    line.append(weight_ref[at, j * BLOCK : (j + 1) * BLOCK] * keep)
                rows.append(jnp.concatenate(line, axis=1))
        pruned = jnp.concatenate(rows, axis=0)
        total += jnp.dot(heads_ref[z], pruned, preferred_element_type=jnp.float32)
    return total


def project_own_kernel(mask_ref, heads_ref, weight_ref, out_ref):
    out_ref[...] = project(mask_ref, heads_ref, weight_ref, lax.axis_index("core"))


def project_other_kernel(mask_ref, heads_ref, weight_ref, part_ref, out_ref):
    rest = project(mask_ref, heads_ref, weight_ref, 1 - lax.axis_index("core"))
    out_ref[...] = (part_ref[...] + rest).astype(out_ref.dtype)


def per_device(queries, keys, values, out_weight, block_mask):
    rows = queries.shape[0]
    columns = out_weight.shape[1]
    half = rows // 2
    mask = block_mask.T
    params = pltpu.CompilerParams(vmem_limit_bytes=32 * 2**20)
    shape = jax.ShapeDtypeStruct
    cost = pl.CostEstimate(flops=2**28, bytes_accessed=2**21, transcendentals=2**19)
    spread = pl.pallas_call(
        spread_kernel,
        out_shape=shape((N_SEQ, half, 2 * HD), jnp.bfloat16),
        in_specs=[ANY] * 2,
        out_specs=VMEM,
        scratch_shapes=[pltpu.VMEM((half, 2 * HD), jnp.bfloat16), pltpu.SemaphoreType.DMA((2,))],
        name="spread_kv",
    )(keys, values)
    swap = [(0, 1), (1, 0)]
    partner_queries = lax.ppermute(queries, "xh", swap)
    own = lax.all_to_all(spread, SEQ, 0, 0, tiled=True)
    other = lax.ppermute(own, "core", swap)
    state = pl.pallas_call(
        attention_first_kernel,
        out_shape=[shape((2 * rows, HD), jnp.float32)] * 3,
        in_specs=[VMEM] * 2,
        out_specs=[VMEM] * 3,
        compiler_params=params,
        cost_estimate=cost,
        name="attention_first",
    )(queries, own)
    own_heads = pl.pallas_call(
        attention_second_kernel,
        out_shape=shape((rows, 2 * HD), jnp.bfloat16),
        in_specs=[VMEM] * 5,
        out_specs=VMEM,
        compiler_params=params,
        cost_estimate=cost,
        name="attention_second",
    )(queries, other, *state)
    heads = pl.pallas_call(
        attention_partner_kernel,
        out_shape=shape((N_Z, rows, 4 * HD), jnp.bfloat16),
        in_specs=[VMEM] * 4,
        out_specs=VMEM,
        compiler_params=params,
        cost_estimate=cost,
        name="attention_partner",
    )(partner_queries, own, other, own_heads)
    own_heads = lax.all_to_all(heads, "z", 0, 0, tiled=True)
    other_heads = lax.ppermute(own_heads, "core", swap)
    part = pl.pallas_call(
        project_own_kernel,
        out_shape=shape((rows, columns), jnp.float32),
        in_specs=[SMEM, VMEM, VMEM],
        out_specs=VMEM,
        compiler_params=params,
        cost_estimate=pl.CostEstimate(flops=2**28, bytes_accessed=2**22, transcendentals=0),
        name="project_own",
    )(mask, own_heads, out_weight)
    return pl.pallas_call(
        project_other_kernel,
        out_shape=shape((rows, columns), jnp.bfloat16),
        in_specs=[SMEM, VMEM, VMEM, VMEM],
        out_specs=VMEM,
        compiler_params=params,
        cost_estimate=pl.CostEstimate(flops=2**28, bytes_accessed=2**22, transcendentals=0),
        name="project_other",
    )(mask, other_heads, out_weight, part)


def solution(mesh):
    fine = Mesh(mesh.devices.reshape(SIZES), AXES)
    return jax.shard_map(
        per_device,
        mesh=fine,
        in_specs=(P(SEQ, FSDP), P(SEQ, None), P(SEQ, None), P(None, FSDP), P(None, FSDP)),
        out_specs=P(SEQ, FSDP),
        check_vma=False,
    )
```

```python
import math

import jax
import jax.numpy as jnp
from jax import lax
from jax.experimental import pallas as pl
from jax.experimental.pallas import tpu as pltpu
from jax.sharding import Mesh
from jax.sharding import PartitionSpec as P

HD = 128
BLOCK = 128
SIZES = (4, 2, 2, 2, 8, 2, 2)
AXES = ("y", "yp", "xl", "xp", "z", "xh", "core")
SEQ = ("y", "yp", "xl", "xp")
SQUARE = ("yp", "xp")
N_SQUARE = 4
FSDP = ("z", "xh", "core")
N_SEQ = 32
N_Z = 8
FACTOR = math.log2(math.e) / math.sqrt(HD)
LOWEST = -1e30
ANY = pl.BlockSpec(memory_space=pl.ANY)
VMEM = pl.BlockSpec(memory_space=pltpu.VMEM)
SMEM = pl.BlockSpec(memory_space=pltpu.SMEM)


def spread_kernel(keys_ref, values_ref, out_ref, block, sems):
    part = out_ref.shape[1]
    column = pl.multiple_of(lax.axis_index("z") * HD, HD)
    core = lax.axis_index("core")
    copies = [
        pltpu.make_async_copy(
            source.at[:, pl.ds(column, HD)], block.at[:, i * HD : (i + 1) * HD], sems.at[i]
        )
        for i, source in enumerate((keys_ref, values_ref))
    ]
    for copy in copies:
        copy.start()
    for copy in copies:
        copy.wait()
    pieces = [
        block[pl.ds(pl.multiple_of((place * 2 + core) * part, part), part), :]
        for place in range(N_SQUARE)
    ]
    for i in range(N_SEQ):
        out_ref[i] = pieces[i // 4 % 2 * 2 + i % 2]


def square_kernel(piece_ref, out_ref):
    for i in range(N_SQUARE):
        out_ref[i] = piece_ref[...]


def attend(queries_ref, kv_ref, from_core, state):
    rows = queries_ref.shape[0]
    part = kv_ref.shape[2]
    width = N_SQUARE * N_SEQ * part
    seq = lax.axis_index("y") * 8 + lax.axis_index("yp") * 4 + lax.axis_index("xl") * 2
    start = (seq + lax.axis_index("xp")) * rows
    q = jnp.concatenate([queries_ref[:, :HD], queries_ref[:, HD:]], axis=0)
    query_pos = start + lax.broadcasted_iota(jnp.int32, (2 * rows, 1), 0) % rows
    column = lax.broadcasted_iota(jnp.int32, (1, width), 1)
    block = column // part
    place = block // N_SEQ * 2 + from_core
    key_pos = block % N_SEQ * rows + place * part + column % part
    key = kv_ref[:, :, :, :HD].reshape(width, HD)
    value = kv_ref[:, :, :, HD:].reshape(width, HD)
    score = lax.dot_general(q, key, (((1,), (1,)), ((), ())), preferred_element_type=jnp.float32)
    score = jnp.where(query_pos >= key_pos, score, jnp.float32(LOWEST))
    top = jnp.max(score, axis=1, keepdims=True)
    if state is not None:
        top = jnp.maximum(state[0], top)
    expo = jnp.exp2((score - top) * FACTOR)
    total = jnp.sum(expo, axis=1, keepdims=True)
    summed = jnp.dot(expo.astype(jnp.bfloat16), value, preferred_element_type=jnp.float32)
    if state is not None:
        fix = jnp.exp2((state[0] - top) * FACTOR)
        total = total + state[1] * fix
        summed = summed + state[2] * fix
    return top, total, summed


def finish(state):
    _, total, summed = state
    rows = total.shape[0] // 2
    normed = (summed / total).astype(jnp.bfloat16)
    return jnp.concatenate([normed[:rows], normed[rows:]], axis=1)


def attention_first_kernel(queries_ref, partner_ref, kv_ref, *state_refs):
    core = lax.axis_index("core")
    for i, queries in enumerate((queries_ref, partner_ref)):
        for ref, value in zip(state_refs, attend(queries, kv_ref, core, None)):
            ref[i] = jnp.broadcast_to(value, ref.shape[1:])


def attention_second_kernel(queries_ref, partner_ref, kv_ref, top_ref, total_ref, summed_ref, out_ref):
    core = lax.axis_index("core")
    heads = []
    for i, queries in enumerate((queries_ref, partner_ref)):
        state = top_ref[i, :, :1], total_ref[i, :, :1], summed_ref[i]
        heads.append(finish(attend(queries, kv_ref, 1 - core, state)))
    heads = jnp.concatenate(heads, axis=1)
    for i in range(N_Z):
        out_ref[i] = heads


def project(mask_ref, heads_ref, weight_ref, from_core):
    columns = weight_ref.shape[1]
    total = jnp.zeros((heads_ref.shape[1], columns), jnp.float32)
    xh = lax.axis_index("xh")
    for z in range(N_Z):
        rows = []
        for chip in (z * 2 + xh, z * 2 + 1 - xh):
            for i in range(2):
                block = (chip * 2 + from_core) * 2 + i
                at = pl.ds(pl.multiple_of(block * BLOCK, BLOCK), BLOCK)
                line = []
                for j in range(columns // BLOCK):
                    keep = mask_ref[j, block].astype(jnp.float32).astype(jnp.bfloat16)
                    line.append(weight_ref[at, j * BLOCK : (j + 1) * BLOCK] * keep)
                rows.append(jnp.concatenate(line, axis=1))
        pruned = jnp.concatenate(rows, axis=0)
        total += jnp.dot(heads_ref[z], pruned, preferred_element_type=jnp.float32)
    return total


def project_own_kernel(mask_ref, heads_ref, weight_ref, out_ref):
    out_ref[...] = project(mask_ref, heads_ref, weight_ref, lax.axis_index("core"))


def project_other_kernel(mask_ref, heads_ref, weight_ref, part_ref, out_ref):
    rest = project(mask_ref, heads_ref, weight_ref, 1 - lax.axis_index("core"))
    out_ref[...] = (part_ref[...] + rest).astype(out_ref.dtype)


def per_device(queries, keys, values, out_weight, block_mask):
    rows = queries.shape[0]
    columns = out_weight.shape[1]
    part = rows // (2 * N_SQUARE)
    mask = block_mask.T
    params = pltpu.CompilerParams(vmem_limit_bytes=32 * 2**20)
    shape = jax.ShapeDtypeStruct
    cost = pl.CostEstimate(flops=2**29, bytes_accessed=2**21, transcendentals=2**20)
    swap = [(0, 1), (1, 0)]
    partner_queries = lax.ppermute(queries, "xh", swap)
    spread = pl.pallas_call(
        spread_kernel,
        out_shape=shape((N_SEQ, part, 2 * HD), jnp.bfloat16),
        in_specs=[ANY] * 2,
        out_specs=VMEM,
        scratch_shapes=[pltpu.VMEM((rows, 2 * HD), jnp.bfloat16), pltpu.SemaphoreType.DMA((2,))],
        name="spread_kv",
    )(keys, values)
    piece = lax.all_to_all(spread, SEQ, 0, 0, tiled=True)
    piece, partner_queries = lax.optimization_barrier((piece, partner_queries))
    square = pl.pallas_call(
        square_kernel,
        out_shape=shape((N_SQUARE, N_SEQ, part, 2 * HD), jnp.bfloat16),
        in_specs=[VMEM],
        out_specs=VMEM,
        compiler_params=params,
        name="square",
    )(piece)
    own = lax.all_to_all(square, SQUARE, 0, 0, tiled=True)
    other = lax.ppermute(own, "core", swap)
    state = pl.pallas_call(
        attention_first_kernel,
        out_shape=[shape((2, 2 * rows, HD), jnp.float32)] * 3,
        in_specs=[VMEM] * 3,
        out_specs=[VMEM] * 3,
        compiler_params=params,
        cost_estimate=cost,
        name="attention_first",
    )(queries, partner_queries, own)
    heads = pl.pallas_call(
        attention_second_kernel,
        out_shape=shape((N_Z, rows, 4 * HD), jnp.bfloat16),
        in_specs=[VMEM] * 6,
        out_specs=VMEM,
        compiler_params=params,
        cost_estimate=cost,
        name="attention_second",
    )(queries, partner_queries, other, *state)
    own_heads = lax.all_to_all(heads, "z", 0, 0, tiled=True)
    other_heads = lax.ppermute(own_heads, "core", swap)
    part = pl.pallas_call(
        project_own_kernel,
        out_shape=shape((rows, columns), jnp.float32),
        in_specs=[SMEM, VMEM, VMEM],
        out_specs=VMEM,
        compiler_params=params,
        cost_estimate=pl.CostEstimate(flops=2**28, bytes_accessed=2**22, transcendentals=0),
        name="project_own",
    )(mask, own_heads, out_weight)
    return pl.pallas_call(
        project_other_kernel,
        out_shape=shape((rows, columns), jnp.bfloat16),
        in_specs=[SMEM, VMEM, VMEM, VMEM],
        out_specs=VMEM,
        compiler_params=params,
        cost_estimate=pl.CostEstimate(flops=2**28, bytes_accessed=2**22, transcendentals=0),
        name="project_other",
    )(mask, other_heads, out_weight, part)


def solution(mesh):
    fine = Mesh(mesh.devices.reshape(SIZES), AXES)
    return jax.shard_map(
        per_device,
        mesh=fine,
        in_specs=(P(SEQ, FSDP), P(SEQ, None), P(SEQ, None), P(None, FSDP), P(None, FSDP)),
        out_specs=P(SEQ, FSDP),
        check_vma=False,
    )
```

```python
import math

import jax
import jax.numpy as jnp
from jax import lax
from jax.experimental import pallas as pl
from jax.experimental.pallas import tpu as pltpu
from jax.sharding import Mesh
from jax.sharding import PartitionSpec as P

HD = 128
BLOCK = 128
SIZES = (4, 2, 2, 2, 8, 2, 2)
AXES = ("y", "yp", "xl", "xp", "z", "xh", "core")
SEQ = ("y", "yp", "xl", "xp")
SQUARE = ("yp", "xp")
N_SQUARE = 4
FSDP = ("z", "xh", "core")
N_SEQ = 32
N_Z = 8
FACTOR = math.log2(math.e) / math.sqrt(HD)
LOWEST = -1e30
ANY = pl.BlockSpec(memory_space=pl.ANY)
VMEM = pl.BlockSpec(memory_space=pltpu.VMEM)
SMEM = pl.BlockSpec(memory_space=pltpu.SMEM)


def spread_kernel(keys_ref, values_ref, out_ref, block, sems):
    part = out_ref.shape[1]
    column = pl.multiple_of(lax.axis_index("z") * HD, HD)
    core = lax.axis_index("core")
    copies = [
        pltpu.make_async_copy(
            source.at[:, pl.ds(column, HD)], block.at[:, i * HD : (i + 1) * HD], sems.at[i]
        )
        for i, source in enumerate((keys_ref, values_ref))
    ]
    for copy in copies:
        copy.start()
    for copy in copies:
        copy.wait()
    pieces = [
        block[pl.ds(pl.multiple_of((place * 2 + core) * part, part), part), :]
        for place in range(N_SQUARE)
    ]
    for i in range(N_SEQ):
        out_ref[i] = pieces[i // 4 % 2 * 2 + i % 2]


def square_kernel(piece_ref, out_ref):
    for i in range(N_SQUARE):
        out_ref[i] = piece_ref[...]


def attend(queries_ref, kv_ref, from_core, state):
    rows = queries_ref.shape[0]
    part = kv_ref.shape[2]
    width = N_SQUARE * N_SEQ * part
    seq = lax.axis_index("y") * 8 + lax.axis_index("yp") * 4 + lax.axis_index("xl") * 2
    start = (seq + lax.axis_index("xp")) * rows
    q = jnp.concatenate([queries_ref[:, :HD], queries_ref[:, HD:]], axis=0)
    query_pos = start + lax.broadcasted_iota(jnp.int32, (2 * rows, 1), 0) % rows
    column = lax.broadcasted_iota(jnp.int32, (1, width), 1)
    block = column // part
    place = block // N_SEQ * 2 + from_core
    key_pos = block % N_SEQ * rows + place * part + column % part
    key = kv_ref[:, :, :, :HD].reshape(width, HD)
    value = kv_ref[:, :, :, HD:].reshape(width, HD)
    score = lax.dot_general(q, key, (((1,), (1,)), ((), ())), preferred_element_type=jnp.float32)
    score = jnp.where(query_pos >= key_pos, score, jnp.float32(LOWEST))
    top = jnp.max(score, axis=1, keepdims=True)
    if state is not None:
        top = jnp.maximum(state[0], top)
    expo = jnp.exp2((score - top) * FACTOR)
    total = jnp.sum(expo, axis=1, keepdims=True)
    summed = jnp.dot(expo.astype(jnp.bfloat16), value, preferred_element_type=jnp.float32)
    if state is not None:
        fix = jnp.exp2((state[0] - top) * FACTOR)
        total = total + state[1] * fix
        summed = summed + state[2] * fix
    return top, total, summed


def finish(state):
    _, total, summed = state
    rows = total.shape[0] // 2
    normed = (summed / total).astype(jnp.bfloat16)
    return jnp.concatenate([normed[:rows], normed[rows:]], axis=1)


def attention_first_kernel(queries_ref, partner_ref, kv_ref, *state_refs):
    core = lax.axis_index("core")
    for i, queries in enumerate((queries_ref, partner_ref)):
        for ref, value in zip(state_refs, attend(queries, kv_ref, core, None)):
            ref[i] = jnp.broadcast_to(value, ref.shape[1:])


def attention_second_kernel(queries_ref, partner_ref, kv_ref, top_ref, total_ref, summed_ref, out_ref):
    core = lax.axis_index("core")
    heads = []
    for i, queries in enumerate((queries_ref, partner_ref)):
        state = top_ref[i, :, :1], total_ref[i, :, :1], summed_ref[i]
        heads.append(finish(attend(queries, kv_ref, 1 - core, state)))
    heads = jnp.concatenate(heads, axis=1)
    for i in range(N_Z):
        out_ref[i] = heads


def project(mask_ref, heads_ref, weight_ref, from_core):
    columns = weight_ref.shape[1]
    total = jnp.zeros((heads_ref.shape[1], columns), jnp.float32)
    xh = lax.axis_index("xh")
    for z in range(N_Z):
        rows = []
        for chip in (z * 2 + xh, z * 2 + 1 - xh):
            for i in range(2):
                block = (chip * 2 + from_core) * 2 + i
                at = pl.ds(pl.multiple_of(block * BLOCK, BLOCK), BLOCK)
                line = []
                for j in range(columns // BLOCK):
                    keep = mask_ref[j, block].astype(jnp.float32).astype(jnp.bfloat16)
                    line.append(weight_ref[at, j * BLOCK : (j + 1) * BLOCK] * keep)
                rows.append(jnp.concatenate(line, axis=1))
        pruned = jnp.concatenate(rows, axis=0)
        total += jnp.dot(heads_ref[z], pruned, preferred_element_type=jnp.float32)
    return total


def project_own_kernel(mask_ref, heads_ref, weight_ref, out_ref):
    out_ref[...] = project(mask_ref, heads_ref, weight_ref, lax.axis_index("core"))


def project_other_kernel(mask_ref, heads_ref, weight_ref, part_ref, out_ref):
    rest = project(mask_ref, heads_ref, weight_ref, 1 - lax.axis_index("core"))
    out_ref[...] = (part_ref[...] + rest).astype(out_ref.dtype)


def per_device(queries, keys, values, out_weight, block_mask):
    rows = queries.shape[0]
    columns = out_weight.shape[1]
    part = rows // (2 * N_SQUARE)
    mask = block_mask.T
    params = pltpu.CompilerParams(vmem_limit_bytes=32 * 2**20)
    shape = jax.ShapeDtypeStruct
    cost = pl.CostEstimate(flops=2**29, bytes_accessed=2**21, transcendentals=2**20)
    swap = [(0, 1), (1, 0)]
    partner_queries = lax.ppermute(queries, "xh", swap)
    spread = pl.pallas_call(
        spread_kernel,
        out_shape=shape((N_SEQ, part, 2 * HD), jnp.bfloat16),
        in_specs=[ANY] * 2,
        out_specs=VMEM,
        scratch_shapes=[pltpu.VMEM((rows, 2 * HD), jnp.bfloat16), pltpu.SemaphoreType.DMA((2,))],
        name="spread_kv",
    )(keys, values)
    piece = lax.all_to_all(spread, SEQ, 0, 0, tiled=True)
    square = pl.pallas_call(
        square_kernel,
        out_shape=shape((N_SQUARE, N_SEQ, part, 2 * HD), jnp.bfloat16),
        in_specs=[VMEM],
        out_specs=VMEM,
        compiler_params=params,
        name="square",
    )(piece)
    own = lax.all_to_all(square, SQUARE, 0, 0, tiled=True)
    own, partner_queries = lax.optimization_barrier((own, partner_queries))
    other = lax.ppermute(own, "core", swap)
    state = pl.pallas_call(
        attention_first_kernel,
        out_shape=[shape((2, 2 * rows, HD), jnp.float32)] * 3,
        in_specs=[VMEM] * 3,
        out_specs=[VMEM] * 3,
        compiler_params=params,
        cost_estimate=cost,
        name="attention_first",
    )(queries, partner_queries, own)
    heads = pl.pallas_call(
        attention_second_kernel,
        out_shape=shape((N_Z, rows, 4 * HD), jnp.bfloat16),
        in_specs=[VMEM] * 6,
        out_specs=VMEM,
        compiler_params=params,
        cost_estimate=cost,
        name="attention_second",
    )(queries, partner_queries, other, *state)
    own_heads = lax.all_to_all(heads, "z", 0, 0, tiled=True)
    other_heads = lax.ppermute(own_heads, "core", swap)
    part = pl.pallas_call(
        project_own_kernel,
        out_shape=shape((rows, columns), jnp.float32),
        in_specs=[SMEM, VMEM, VMEM],
        out_specs=VMEM,
        compiler_params=params,
        cost_estimate=pl.CostEstimate(flops=2**28, bytes_accessed=2**22, transcendentals=0),
        name="project_own",
    )(mask, own_heads, out_weight)
    return pl.pallas_call(
        project_other_kernel,
        out_shape=shape((rows, columns), jnp.bfloat16),
        in_specs=[SMEM, VMEM, VMEM, VMEM],
        out_specs=VMEM,
        compiler_params=params,
        cost_estimate=pl.CostEstimate(flops=2**28, bytes_accessed=2**22, transcendentals=0),
        name="project_other",
    )(mask, other_heads, out_weight, part)


def solution(mesh):
    fine = Mesh(mesh.devices.reshape(SIZES), AXES)
    return jax.shard_map(
        per_device,
        mesh=fine,
        in_specs=(P(SEQ, FSDP), P(SEQ, None), P(SEQ, None), P(None, FSDP), P(None, FSDP)),
        out_specs=P(SEQ, FSDP),
        check_vma=False,
    )
```

```python
import functools
import math

import jax
import jax.numpy as jnp
from jax import lax
from jax.experimental import pallas as pl
from jax.experimental.pallas import tpu as pltpu
from jax.sharding import Mesh
from jax.sharding import PartitionSpec as P

HD = 128
BLOCK = 128
SIZES = (4, 2, 2, 2, 8, 2, 2)
AXES = ("y", "yp", "xl", "xp", "z", "xh", "core")
SEQ = ("y", "yp", "xl", "xp")
SQUARE = ("yp", "xp")
N_SQUARE = 4
FSDP = ("z", "xh", "core")
N_SEQ = 32
N_Z = 8
FACTOR = math.log2(math.e) / math.sqrt(HD)
LOWEST = -1e30
ANY = pl.BlockSpec(memory_space=pl.ANY)
VMEM = pl.BlockSpec(memory_space=pltpu.VMEM)
SMEM = pl.BlockSpec(memory_space=pltpu.SMEM)


def spread_kernel(keys_ref, values_ref, out_ref, block, sems):
    part = out_ref.shape[1]
    column = pl.multiple_of(lax.axis_index("z") * HD, HD)
    core = lax.axis_index("core")
    copies = [
        pltpu.make_async_copy(
            source.at[:, pl.ds(column, HD)], block.at[:, i * HD : (i + 1) * HD], sems.at[i]
        )
        for i, source in enumerate((keys_ref, values_ref))
    ]
    for copy in copies:
        copy.start()
    for copy in copies:
        copy.wait()
    pieces = [
        block[pl.ds(pl.multiple_of((place * 2 + core) * part, part), part), :]
        for place in range(N_SQUARE)
    ]
    for i in range(N_SEQ):
        out_ref[i] = pieces[i // 4 % 2 * 2 + i % 2]


def square_kernel(piece_ref, out_ref):
    for i in range(N_SQUARE):
        out_ref[i] = piece_ref[...]


def attend(queries_ref, kv_ref, from_core, state):
    rows = queries_ref.shape[0]
    part = kv_ref.shape[2]
    width = N_SQUARE * N_SEQ * part
    seq = lax.axis_index("y") * 8 + lax.axis_index("yp") * 4 + lax.axis_index("xl") * 2
    start = (seq + lax.axis_index("xp")) * rows
    q = jnp.concatenate([queries_ref[:, :HD], queries_ref[:, HD:]], axis=0)
    query_pos = start + lax.broadcasted_iota(jnp.int32, (2 * rows, 1), 0) % rows
    column = lax.broadcasted_iota(jnp.int32, (1, width), 1)
    block = column // part
    place = block // N_SEQ * 2 + from_core
    key_pos = block % N_SEQ * rows + place * part + column % part
    key = kv_ref[:, :, :, :HD].reshape(width, HD)
    value = kv_ref[:, :, :, HD:].reshape(width, HD)
    score = lax.dot_general(q, key, (((1,), (1,)), ((), ())), preferred_element_type=jnp.float32)
    score = jnp.where(query_pos >= key_pos, score, jnp.float32(LOWEST))
    top = jnp.max(score, axis=1, keepdims=True)
    if state is not None:
        top = jnp.maximum(state[0], top)
    expo = jnp.exp2((score - top) * FACTOR)
    total = jnp.sum(expo, axis=1, keepdims=True)
    summed = jnp.dot(expo.astype(jnp.bfloat16), value, preferred_element_type=jnp.float32)
    if state is not None:
        fix = jnp.exp2((state[0] - top) * FACTOR)
        total = total + state[1] * fix
        summed = summed + state[2] * fix
    return top, total, summed


def finish(state):
    _, total, summed = state
    rows = total.shape[0] // 2
    normed = (summed / total).astype(jnp.bfloat16)
    return jnp.concatenate([normed[:rows], normed[rows:]], axis=1)


def attention_first_kernel(queries_ref, partner_ref, kv_ref, *state_refs):
    core = lax.axis_index("core")
    for i, queries in enumerate((queries_ref, partner_ref)):
        for ref, value in zip(state_refs, attend(queries, kv_ref, core, None)):
            ref[i] = jnp.broadcast_to(value, ref.shape[1:])


def attention_second_kernel(which, queries_ref, kv_ref, top_ref, total_ref, summed_ref, out_ref):
    state = top_ref[which, :, :1], total_ref[which, :, :1], summed_ref[which]
    heads = finish(attend(queries_ref, kv_ref, 1 - lax.axis_index("core"), state))
    for i in range(N_Z):
        out_ref[i] = heads


def project(mask_ref, heads_ref, weight_ref, from_chip, from_core):
    columns = weight_ref.shape[1]
    total = jnp.zeros((heads_ref.shape[1], columns), jnp.float32)
    for z in range(N_Z):
        rows = []
        for i in range(2):
            block = ((z * 2 + from_chip) * 2 + from_core) * 2 + i
            at = pl.ds(pl.multiple_of(block * BLOCK, BLOCK), BLOCK)
            line = []
            for j in range(columns // BLOCK):
                keep = mask_ref[j, block].astype(jnp.float32).astype(jnp.bfloat16)
                line.append(weight_ref[at, j * BLOCK : (j + 1) * BLOCK] * keep)
            rows.append(jnp.concatenate(line, axis=1))
        pruned = jnp.concatenate(rows, axis=0)
        total += jnp.dot(heads_ref[z], pruned, preferred_element_type=jnp.float32)
    return total


def project_kernel(of_partner, of_sibling, mask_ref, heads_ref, weight_ref, *refs):
    xh, core = lax.axis_index("xh"), lax.axis_index("core")
    part = project(
        mask_ref, heads_ref, weight_ref, 1 - xh if of_partner else xh, 1 - core if of_sibling else core
    )
    out_ref = refs[-1]
    for before_ref in refs[:-1]:
        part = part + before_ref[...]
    out_ref[...] = part.astype(out_ref.dtype)


def per_device(queries, keys, values, out_weight, block_mask):
    rows = queries.shape[0]
    columns = out_weight.shape[1]
    part = rows // (2 * N_SQUARE)
    mask = block_mask.T
    params = pltpu.CompilerParams(vmem_limit_bytes=32 * 2**20)
    shape = jax.ShapeDtypeStruct
    cost = pl.CostEstimate(flops=2**29, bytes_accessed=2**21, transcendentals=2**20)
    swap = [(0, 1), (1, 0)]
    partner_queries = lax.ppermute(queries, "xh", swap)
    spread = pl.pallas_call(
        spread_kernel,
        out_shape=shape((N_SEQ, part, 2 * HD), jnp.bfloat16),
        in_specs=[ANY] * 2,
        out_specs=VMEM,
        scratch_shapes=[pltpu.VMEM((rows, 2 * HD), jnp.bfloat16), pltpu.SemaphoreType.DMA((2,))],
        name="spread_kv",
    )(keys, values)
    piece = lax.all_to_all(spread, SEQ, 0, 0, tiled=True)
    piece, partner_queries = lax.optimization_barrier((piece, partner_queries))
    square = pl.pallas_call(
        square_kernel,
        out_shape=shape((N_SQUARE, N_SEQ, part, 2 * HD), jnp.bfloat16),
        in_specs=[VMEM],
        out_specs=VMEM,
        compiler_params=params,
        name="square",
    )(piece)
    own = lax.all_to_all(square, SQUARE, 0, 0, tiled=True)
    other = lax.ppermute(own, "core", swap)
    state = pl.pallas_call(
        attention_first_kernel,
        out_shape=[shape((2, 2 * rows, HD), jnp.float32)] * 3,
        in_specs=[VMEM] * 3,
        out_specs=[VMEM] * 3,
        compiler_params=params,
        cost_estimate=cost,
        name="attention_first",
    )(queries, partner_queries, own)
    parts = []
    for which, (name, its_queries) in enumerate((("own", queries), ("partner", partner_queries))):
        heads = pl.pallas_call(
            functools.partial(attention_second_kernel, which),
            out_shape=shape((N_Z, rows, 2 * HD), jnp.bfloat16),
            in_specs=[VMEM] * 5,
            out_specs=VMEM,
            compiler_params=params,
            cost_estimate=cost,
            name="attention_second_" + name,
        )(its_queries, other, *state)
        along_z = lax.all_to_all(heads, "z", 0, 0, tiled=True)
        sibling = lax.ppermute(along_z, "core", swap)
        for of_sibling, got in enumerate((along_z, sibling)):
            last = which and of_sibling
            parts = [
                pl.pallas_call(
                    functools.partial(project_kernel, which, of_sibling),
                    out_shape=shape((rows, columns), jnp.bfloat16 if last else jnp.float32),
                    in_specs=[SMEM] + [VMEM] * (2 + len(parts)),
                    out_specs=VMEM,
                    compiler_params=params,
                    cost_estimate=pl.CostEstimate(
                        flops=2**27, bytes_accessed=2**21, transcendentals=0
                    ),
                    name="project_" + name + "_" + ("sibling" if of_sibling else "self"),
                )(mask, got, out_weight, *parts)
            ]
    return parts[0]


def solution(mesh):
    fine = Mesh(mesh.devices.reshape(SIZES), AXES)
    return jax.shard_map(
        per_device,
        mesh=fine,
        in_specs=(P(SEQ, FSDP), P(SEQ, None), P(SEQ, None), P(None, FSDP), P(None, FSDP)),
        out_specs=P(SEQ, FSDP),
        check_vma=False,
    )
```

```python
import math

import jax
import jax.numpy as jnp
from jax import lax
from jax.experimental import pallas as pl
from jax.experimental.pallas import tpu as pltpu
from jax.sharding import Mesh
from jax.sharding import PartitionSpec as P

HD = 128
BLOCK = 128
SIZES = (4, 2, 2, 2, 8, 2, 2)
AXES = ("y", "yp", "xl", "xp", "z", "xh", "core")
SEQ = ("y", "yp", "xl", "xp")
N_SQUARE = 4
PLANE = ("y", "yp", "xl", "xp", "xh", "core")
RING = ("z", "core")
FSDP = ("z", "xh", "core")
N_SEQ = 32
N_Z = 8
FACTOR = math.log2(math.e) / math.sqrt(HD)
LOWEST = -1e30
ANY = pl.BlockSpec(memory_space=pl.ANY)
VMEM = pl.BlockSpec(memory_space=pltpu.VMEM)
SMEM = pl.BlockSpec(memory_space=pltpu.SMEM)


def square_groups():
    groups = []
    for core in range(2):
        for top in range(core, 8, 2):
            for left in range(core, 8, 2):
                group = [None] * N_SQUARE
                for y in (top, (top + 1) % 8):
                    for x in (left, (left + 1) % 8):
                        flat = (y * 4 + x % 4) * 2 + x // 4
                        group[y % 2 * 2 + x % 2] = flat * 2 + core
                groups.append(group)
    return groups


def z_pairs():
    pairs = []
    for z in range(8):
        for core in range(2):
            other = z ^ 1 if core == 0 else (((z + 1) ^ 1) - 1) % 8
            pairs.append((z * 2 + core, other * 2 + core))
    return pairs


def spread_kernel(keys_ref, values_ref, out_ref, block, sems):
    part = out_ref.shape[1]
    column = pl.multiple_of(lax.axis_index("z") * HD, HD)
    core = lax.axis_index("core")
    copies = [
        pltpu.make_async_copy(
            source.at[:, pl.ds(column, HD)], block.at[:, i * HD : (i + 1) * HD], sems.at[i]
        )
        for i, source in enumerate((keys_ref, values_ref))
    ]
    for copy in copies:
        copy.start()
    for copy in copies:
        copy.wait()
    pieces = [
        block[pl.ds(pl.multiple_of((place * 2 + core) * part, part), part), :]
        for place in range(N_SQUARE)
    ]
    for i in range(N_SEQ):
        out_ref[i] = pieces[i // 4 % 2 * 2 + i % 2]


def square_kernel(piece_ref, out_ref):
    for i in range(N_SQUARE):
        out_ref[i] = piece_ref[...]


def attend(queries_ref, kv_ref, from_core, state):
    rows = queries_ref.shape[0]
    part = kv_ref.shape[2]
    width = N_SQUARE * N_SEQ * part
    seq = lax.axis_index("y") * 8 + lax.axis_index("yp") * 4 + lax.axis_index("xl") * 2
    start = (seq + lax.axis_index("xp")) * rows
    q = jnp.concatenate([queries_ref[:, :HD], queries_ref[:, HD:]], axis=0)
    query_pos = start + lax.broadcasted_iota(jnp.int32, (2 * rows, 1), 0) % rows
    column = lax.broadcasted_iota(jnp.int32, (1, width), 1)
    block = column // part
    place = block // N_SEQ * 2 + from_core
    key_pos = block % N_SEQ * rows + place * part + column % part
    key = kv_ref[:, :, :, :HD].reshape(width, HD)
    value = kv_ref[:, :, :, HD:].reshape(width, HD)
    score = lax.dot_general(q, key, (((1,), (1,)), ((), ())), preferred_element_type=jnp.float32)
    score = jnp.where(query_pos >= key_pos, score, jnp.float32(LOWEST))
    top = jnp.max(score, axis=1, keepdims=True)
    if state is not None:
        top = jnp.maximum(state[0], top)
    expo = jnp.exp2((score - top) * FACTOR)
    total = jnp.sum(expo, axis=1, keepdims=True)
    summed = jnp.dot(expo.astype(jnp.bfloat16), value, preferred_element_type=jnp.float32)
    if state is not None:
        fix = jnp.exp2((state[0] - top) * FACTOR)
        total = total + state[1] * fix
        summed = summed + state[2] * fix
    return top, total, summed


def finish(state):
    _, total, summed = state
    rows = total.shape[0] // 2
    normed = (summed / total).astype(jnp.bfloat16)
    return jnp.concatenate([normed[:rows], normed[rows:]], axis=1)


def attention_first_kernel(queries_ref, partner_ref, kv_ref, *state_refs):
    core = lax.axis_index("core")
    for i, queries in enumerate((queries_ref, partner_ref)):
        for ref, value in zip(state_refs, attend(queries, kv_ref, core, None)):
            ref[i] = jnp.broadcast_to(value, ref.shape[1:])


def attention_second_kernel(queries_ref, partner_ref, kv_ref, top_ref, total_ref, summed_ref, out_ref):
    core = lax.axis_index("core")
    heads = []
    for i, queries in enumerate((queries_ref, partner_ref)):
        state = top_ref[i, :, :1], total_ref[i, :, :1], summed_ref[i]
        heads.append(finish(attend(queries, kv_ref, 1 - core, state)))
    first = lax.axis_index("xh") == 0
    heads = [jnp.where(first, heads[0], heads[1]), jnp.where(first, heads[1], heads[0])]
    for i in range(N_Z):
        out_ref[i] = heads[i % 2]


def project(mask_ref, heads_ref, weight_ref, of_pair, of_sibling):
    columns = weight_ref.shape[1]
    parity, core = lax.rem(lax.axis_index("z"), 2), lax.axis_index("core")
    from_chip = 1 - parity if of_pair else parity
    from_core = 1 - core if of_sibling else core
    total = jnp.zeros((heads_ref.shape[1], columns), jnp.float32)
    for z in range(N_Z):
        rows = []
        for i in range(2):
            block = ((z * 2 + from_chip) * 2 + from_core) * 2 + i
            at = pl.ds(pl.multiple_of(block * BLOCK, BLOCK), BLOCK)
            line = []
            for j in range(columns // BLOCK):
                keep = mask_ref[j, block].astype(jnp.float32).astype(jnp.bfloat16)
                line.append(weight_ref[at, j * BLOCK : (j + 1) * BLOCK] * keep)
            rows.append(jnp.concatenate(line, axis=1))
        pruned = jnp.concatenate(rows, axis=0)
        total += jnp.dot(heads_ref[z], pruned, preferred_element_type=jnp.float32)
    return total


def project_first_kernel(mask_ref, weight_ref, self_ref, out_ref):
    out_ref[...] = project(mask_ref, self_ref, weight_ref, False, False)


def project_second_kernel(mask_ref, weight_ref, sibling_ref, pair_ref, part_ref, out_ref):
    part = part_ref[...] + project(mask_ref, sibling_ref, weight_ref, False, True)
    out_ref[...] = part + project(mask_ref, pair_ref, weight_ref, True, False)


def project_third_kernel(mask_ref, weight_ref, sibling_ref, part_ref, out_ref):
    part = part_ref[...] + project(mask_ref, sibling_ref, weight_ref, True, True)
    out_ref[...] = part.astype(out_ref.dtype)


def per_device(queries, keys, values, out_weight, block_mask):
    rows = queries.shape[0]
    columns = out_weight.shape[1]
    part = rows // (2 * N_SQUARE)
    mask = block_mask.T
    params = pltpu.CompilerParams(vmem_limit_bytes=32 * 2**20)
    shape = jax.ShapeDtypeStruct
    cost = pl.CostEstimate(flops=2**29, bytes_accessed=2**21, transcendentals=2**20)
    swap = [(0, 1), (1, 0)]
    partner_queries = lax.ppermute(queries, "xh", swap)
    spread = pl.pallas_call(
        spread_kernel,
        out_shape=shape((N_SEQ, part, 2 * HD), jnp.bfloat16),
        in_specs=[ANY] * 2,
        out_specs=VMEM,
        scratch_shapes=[pltpu.VMEM((rows, 2 * HD), jnp.bfloat16), pltpu.SemaphoreType.DMA((2,))],
        name="spread_kv",
    )(keys, values)
    piece = lax.all_to_all(spread, SEQ, 0, 0, tiled=True)
    piece, partner_queries = lax.optimization_barrier((piece, partner_queries))
    square = pl.pallas_call(
        square_kernel,
        out_shape=shape((N_SQUARE, N_SEQ, part, 2 * HD), jnp.bfloat16),
        in_specs=[VMEM],
        out_specs=VMEM,
        compiler_params=params,
        name="square",
    )(piece)
    own = lax.all_to_all(square, PLANE, 0, 0, axis_index_groups=square_groups(), tiled=True)
    other = lax.ppermute(own, "core", swap)
    state = pl.pallas_call(
        attention_first_kernel,
        out_shape=[shape((2, 2 * rows, HD), jnp.float32)] * 3,
        in_specs=[VMEM] * 3,
        out_specs=[VMEM] * 3,
        compiler_params=params,
        cost_estimate=cost,
        name="attention_first",
    )(queries, partner_queries, own)
    heads = pl.pallas_call(
        attention_second_kernel,
        out_shape=shape((N_Z, rows, 2 * HD), jnp.bfloat16),
        in_specs=[VMEM] * 6,
        out_specs=VMEM,
        compiler_params=params,
        cost_estimate=cost,
        name="attention_second",
    )(queries, partner_queries, other, *state)
    along_z = lax.all_to_all(heads, "z", 0, 0, tiled=True)
    from_pair = lax.ppermute(along_z, RING, z_pairs())
    sibling = lax.ppermute(along_z, "core", swap)
    pair_sibling = lax.ppermute(from_pair, "core", swap)

    def call(kernel, name, dtype, *arrays):
        return pl.pallas_call(
            kernel,
            out_shape=shape((rows, columns), dtype),
            in_specs=[SMEM] + [VMEM] * (1 + len(arrays)),
            out_specs=VMEM,
            compiler_params=params,
            cost_estimate=pl.CostEstimate(flops=2**27, bytes_accessed=2**21, transcendentals=0),
            name=name,
        )(mask, out_weight, *arrays)

    first = call(project_first_kernel, "project_first", jnp.float32, along_z)
    second = call(project_second_kernel, "project_second", jnp.float32, sibling, from_pair, first)
    return call(project_third_kernel, "project_third", jnp.bfloat16, pair_sibling, second)


def solution(mesh):
    fine = Mesh(mesh.devices.reshape(SIZES), AXES)
    return jax.shard_map(
        per_device,
        mesh=fine,
        in_specs=(P(SEQ, FSDP), P(SEQ, None), P(SEQ, None), P(None, FSDP), P(None, FSDP)),
        out_specs=P(SEQ, FSDP),
        check_vma=False,
    )
```

```python
import math

import jax
import jax.numpy as jnp
from jax import lax
from jax.experimental import pallas as pl
from jax.experimental.pallas import tpu as pltpu
from jax.sharding import Mesh
from jax.sharding import PartitionSpec as P

HD = 128
BLOCK = 128
SIZES = (4, 2, 2, 2, 8, 2, 2)
AXES = ("y", "yp", "xl", "xp", "z", "xh", "core")
SEQ = ("y", "yp", "xl", "xp")
N_PAIR = 2
COLUMN = ("y", "yp", "core")
RING = ("z", "core")
FSDP = ("z", "xh", "core")
N_SEQ = 32
N_Z = 8
FACTOR = math.log2(math.e) / math.sqrt(HD)
LOWEST = -1e30
ANY = pl.BlockSpec(memory_space=pl.ANY)
VMEM = pl.BlockSpec(memory_space=pltpu.VMEM)
SMEM = pl.BlockSpec(memory_space=pltpu.SMEM)


def y_pairs():
    groups = []
    for core in range(2):
        for first in range(core, 8, 2):
            members = sorted((first, (first + 1) % 8), key=lambda y: y % 2)
            groups.append([y * 2 + core for y in members])
    return groups


def z_pairs():
    pairs = []
    for z in range(8):
        for core in range(2):
            other = z ^ 1 if core == 0 else (((z + 1) ^ 1) - 1) % 8
            pairs.append((z * 2 + core, other * 2 + core))
    return pairs


def spread_kernel(keys_ref, values_ref, out_ref, block, sems):
    part = out_ref.shape[1]
    column = pl.multiple_of(lax.axis_index("z") * HD, HD)
    core = lax.axis_index("core")
    copies = [
        pltpu.make_async_copy(
            source.at[:, pl.ds(column, HD)], block.at[:, i * HD : (i + 1) * HD], sems.at[i]
        )
        for i, source in enumerate((keys_ref, values_ref))
    ]
    for copy in copies:
        copy.start()
    for copy in copies:
        copy.wait()
    pieces = [
        block[pl.ds(pl.multiple_of((place * 2 + core) * part, part), part), :]
        for place in range(N_PAIR)
    ]
    for i in range(N_SEQ):
        out_ref[i] = pieces[i // 4 % 2]


def pair_kernel(piece_ref, out_ref):
    for i in range(N_PAIR):
        out_ref[i] = piece_ref[...]


def attend(queries_ref, kv_ref, from_core, state):
    rows = queries_ref.shape[0]
    part = kv_ref.shape[2]
    width = N_PAIR * N_SEQ * part
    seq = lax.axis_index("y") * 8 + lax.axis_index("yp") * 4 + lax.axis_index("xl") * 2
    start = (seq + lax.axis_index("xp")) * rows
    q = jnp.concatenate([queries_ref[:, :HD], queries_ref[:, HD:]], axis=0)
    query_pos = start + lax.broadcasted_iota(jnp.int32, (2 * rows, 1), 0) % rows
    column = lax.broadcasted_iota(jnp.int32, (1, width), 1)
    block = column // part
    place = block // N_SEQ * 2 + from_core
    key_pos = block % N_SEQ * rows + place * part + column % part
    key = kv_ref[:, :, :, :HD].reshape(width, HD)
    value = kv_ref[:, :, :, HD:].reshape(width, HD)
    score = lax.dot_general(q, key, (((1,), (1,)), ((), ())), preferred_element_type=jnp.float32)
    score = jnp.where(query_pos >= key_pos, score, jnp.float32(LOWEST))
    top = jnp.max(score, axis=1, keepdims=True)
    if state is not None:
        top = jnp.maximum(state[0], top)
    expo = jnp.exp2((score - top) * FACTOR)
    total = jnp.sum(expo, axis=1, keepdims=True)
    summed = jnp.dot(expo.astype(jnp.bfloat16), value, preferred_element_type=jnp.float32)
    if state is not None:
        fix = jnp.exp2((state[0] - top) * FACTOR)
        total = total + state[1] * fix
        summed = summed + state[2] * fix
    return top, total, summed


def finish(state):
    _, total, summed = state
    rows = total.shape[0] // 2
    normed = (summed / total).astype(jnp.bfloat16)
    return jnp.concatenate([normed[:rows], normed[rows:]], axis=1)


def attention_first_kernel(queries_ref, partner_ref, kv_ref, *state_refs):
    core = lax.axis_index("core")
    for i, queries in enumerate((queries_ref, partner_ref)):
        for ref, value in zip(state_refs, attend(queries, kv_ref, core, None)):
            ref[i] = jnp.broadcast_to(value, ref.shape[1:])


def attention_second_kernel(queries_ref, partner_ref, kv_ref, top_ref, total_ref, summed_ref, out_ref):
    core = lax.axis_index("core")
    heads = []
    for i, queries in enumerate((queries_ref, partner_ref)):
        state = top_ref[i, :, :1], total_ref[i, :, :1], summed_ref[i]
        heads.append(finish(attend(queries, kv_ref, 1 - core, state)))
    first = lax.axis_index("xh") == 0
    heads = [jnp.where(first, heads[0], heads[1]), jnp.where(first, heads[1], heads[0])]
    for i in range(N_Z):
        out_ref[i] = heads[i % 2]


def project(mask_ref, heads_ref, weight_ref, of_pair, of_sibling):
    columns = weight_ref.shape[1]
    parity, core = lax.rem(lax.axis_index("z"), 2), lax.axis_index("core")
    from_chip = 1 - parity if of_pair else parity
    from_core = 1 - core if of_sibling else core
    total = jnp.zeros((heads_ref.shape[1], columns), jnp.float32)
    for z in range(N_Z):
        rows = []
        for i in range(2):
            block = ((z * 2 + from_chip) * 2 + from_core) * 2 + i
            at = pl.ds(pl.multiple_of(block * BLOCK, BLOCK), BLOCK)
            line = []
            for j in range(columns // BLOCK):
                keep = mask_ref[j, block].astype(jnp.float32).astype(jnp.bfloat16)
                line.append(weight_ref[at, j * BLOCK : (j + 1) * BLOCK] * keep)
            rows.append(jnp.concatenate(line, axis=1))
        pruned = jnp.concatenate(rows, axis=0)
        total += jnp.dot(heads_ref[z], pruned, preferred_element_type=jnp.float32)
    return total


def project_first_kernel(mask_ref, weight_ref, self_ref, out_ref):
    out_ref[...] = project(mask_ref, self_ref, weight_ref, False, False)


def project_second_kernel(mask_ref, weight_ref, sibling_ref, pair_ref, part_ref, out_ref):
    part = part_ref[...] + project(mask_ref, sibling_ref, weight_ref, False, True)
    out_ref[...] = part + project(mask_ref, pair_ref, weight_ref, True, False)


def project_third_kernel(mask_ref, weight_ref, sibling_ref, part_ref, out_ref):
    part = part_ref[...] + project(mask_ref, sibling_ref, weight_ref, True, True)
    out_ref[...] = part.astype(out_ref.dtype)


def per_device(queries, keys, values, out_weight, block_mask):
    rows = queries.shape[0]
    columns = out_weight.shape[1]
    part = rows // (2 * N_PAIR)
    mask = block_mask.T
    params = pltpu.CompilerParams(vmem_limit_bytes=32 * 2**20)
    shape = jax.ShapeDtypeStruct
    cost = pl.CostEstimate(flops=2**29, bytes_accessed=2**21, transcendentals=2**20)
    swap = [(0, 1), (1, 0)]
    partner_queries = lax.ppermute(queries, "xh", swap)
    spread = pl.pallas_call(
        spread_kernel,
        out_shape=shape((N_SEQ, part, 2 * HD), jnp.bfloat16),
        in_specs=[ANY] * 2,
        out_specs=VMEM,
        scratch_shapes=[pltpu.VMEM((rows, 2 * HD), jnp.bfloat16), pltpu.SemaphoreType.DMA((2,))],
        name="spread_kv",
    )(keys, values)
    piece = lax.all_to_all(spread, SEQ, 0, 0, tiled=True)
    piece, partner_queries = lax.optimization_barrier((piece, partner_queries))
    pair = pl.pallas_call(
        pair_kernel,
        out_shape=shape((N_PAIR, N_SEQ, part, 2 * HD), jnp.bfloat16),
        in_specs=[VMEM],
        out_specs=VMEM,
        compiler_params=params,
        name="pair",
    )(piece)
    own = lax.all_to_all(pair, COLUMN, 0, 0, axis_index_groups=y_pairs(), tiled=True)
    other = lax.ppermute(own, "core", swap)
    state = pl.pallas_call(
        attention_first_kernel,
        out_shape=[shape((2, 2 * rows, HD), jnp.float32)] * 3,
        in_specs=[VMEM] * 3,
        out_specs=[VMEM] * 3,
        compiler_params=params,
        cost_estimate=cost,
        name="attention_first",
    )(queries, partner_queries, own)
    heads = pl.pallas_call(
        attention_second_kernel,
        out_shape=shape((N_Z, rows, 2 * HD), jnp.bfloat16),
        in_specs=[VMEM] * 6,
        out_specs=VMEM,
        compiler_params=params,
        cost_estimate=cost,
        name="attention_second",
    )(queries, partner_queries, other, *state)
    along_z = lax.all_to_all(heads, "z", 0, 0, tiled=True)
    from_pair = lax.ppermute(along_z, RING, z_pairs())
    sibling = lax.ppermute(along_z, "core", swap)

    def call(kernel, name, dtype, *arrays):
        return pl.pallas_call(
            kernel,
            out_shape=shape((rows, columns), dtype),
            in_specs=[SMEM] + [VMEM] * (1 + len(arrays)),
            out_specs=VMEM,
            compiler_params=params,
            cost_estimate=pl.CostEstimate(flops=2**27, bytes_accessed=2**21, transcendentals=0),
            name=name,
        )(mask, out_weight, *arrays)

    first = call(project_first_kernel, "project_first", jnp.float32, along_z)
    from_pair, first = lax.optimization_barrier((from_pair, first))
    pair_sibling = lax.ppermute(from_pair, "core", swap)
    second = call(project_second_kernel, "project_second", jnp.float32, sibling, from_pair, first)
    return call(project_third_kernel, "project_third", jnp.bfloat16, pair_sibling, second)


def solution(mesh):
    fine = Mesh(mesh.devices.reshape(SIZES), AXES)
    return jax.shard_map(
        per_device,
        mesh=fine,
        in_specs=(P(SEQ, FSDP), P(SEQ, None), P(SEQ, None), P(None, FSDP), P(None, FSDP)),
        out_specs=P(SEQ, FSDP),
        check_vma=False,
    )
```

```python
import math

import jax
import jax.numpy as jnp
from jax import lax
from jax.experimental import pallas as pl
from jax.experimental.pallas import tpu as pltpu
from jax.sharding import Mesh
from jax.sharding import PartitionSpec as P

HD = 128
BLOCK = 128
SIZES = (4, 2, 2, 2, 8, 2, 2)
AXES = ("y", "yp", "xl", "xp", "z", "xh", "core")
SEQ = ("y", "yp", "xl", "xp")
N_SQUARE = 4
PLANE = ("y", "yp", "xl", "xp", "xh", "core")
RING = ("z", "core")
FSDP = ("z", "xh", "core")
N_SEQ = 32
N_Z = 8
FACTOR = math.log2(math.e) / math.sqrt(HD)
LOWEST = -1e30
ANY = pl.BlockSpec(memory_space=pl.ANY)
VMEM = pl.BlockSpec(memory_space=pltpu.VMEM)
SMEM = pl.BlockSpec(memory_space=pltpu.SMEM)


def square_groups():
    groups = []
    for core in range(2):
        for top in range(core, 8, 2):
            for left in range(core, 8, 2):
                group = [None] * N_SQUARE
                for y in (top, (top + 1) % 8):
                    for x in (left, (left + 1) % 8):
                        flat = (y * 4 + x % 4) * 2 + x // 4
                        group[y % 2 * 2 + x % 2] = flat * 2 + core
                groups.append(group)
    return groups


def z_pairs():
    pairs = []
    for z in range(8):
        for core in range(2):
            other = z ^ 1 if core == 0 else (((z + 1) ^ 1) - 1) % 8
            pairs.append((z * 2 + core, other * 2 + core))
    return pairs


def spread_kernel(keys_ref, values_ref, out_ref, block, sems):
    part = out_ref.shape[1]
    column = pl.multiple_of(lax.axis_index("z") * HD, HD)
    core = lax.axis_index("core")
    copies = [
        pltpu.make_async_copy(
            source.at[:, pl.ds(column, HD)], block.at[:, i * HD : (i + 1) * HD], sems.at[i]
        )
        for i, source in enumerate((keys_ref, values_ref))
    ]
    for copy in copies:
        copy.start()
    for copy in copies:
        copy.wait()
    pieces = [
        block[pl.ds(pl.multiple_of((place * 2 + core) * part, part), part), :]
        for place in range(N_SQUARE)
    ]
    for i in range(N_SEQ):
        out_ref[i] = pieces[i // 4 % 2 * 2 + i % 2]


def square_kernel(piece_ref, out_ref):
    for i in range(N_SQUARE):
        out_ref[i] = piece_ref[...]


def stack_kernel(queries_ref, partner_ref, out_ref):
    rows = queries_ref.shape[0]
    for i, ref in enumerate((queries_ref, partner_ref)):
        for head in range(2):
            out_ref[i, head * rows : (head + 1) * rows] = ref[:, head * HD : (head + 1) * HD]


def attend(q, kv_ref, from_core, state):
    rows = q.shape[0] // 2
    part = kv_ref.shape[2]
    width = N_SQUARE * N_SEQ * part
    seq = lax.axis_index("y") * 8 + lax.axis_index("yp") * 4 + lax.axis_index("xl") * 2
    start = (seq + lax.axis_index("xp")) * rows
    query_pos = start + lax.broadcasted_iota(jnp.int32, (2 * rows, 1), 0) % rows
    column = lax.broadcasted_iota(jnp.int32, (1, width), 1)
    block = column // part
    place = block // N_SEQ * 2 + from_core
    key_pos = block % N_SEQ * rows + place * part + column % part
    key = kv_ref[:, :, :, :HD].reshape(width, HD)
    value = kv_ref[:, :, :, HD:].reshape(width, HD)
    score = lax.dot_general(q, key, (((1,), (1,)), ((), ())), preferred_element_type=jnp.float32)
    score = jnp.where(query_pos >= key_pos, score, jnp.float32(LOWEST))
    top = jnp.max(score, axis=1, keepdims=True)
    if state is not None:
        top = jnp.maximum(state[0], top)
    expo = jnp.exp2((score - top) * FACTOR)
    total = jnp.sum(expo, axis=1, keepdims=True)
    summed = jnp.dot(expo.astype(jnp.bfloat16), value, preferred_element_type=jnp.float32)
    if state is not None:
        fix = jnp.exp2((state[0] - top) * FACTOR)
        total = total + state[1] * fix
        summed = summed + state[2] * fix
    return top, total, summed


def finish(state):
    _, total, summed = state
    rows = total.shape[0] // 2
    normed = (summed / total).astype(jnp.bfloat16)
    return jnp.concatenate([normed[:rows], normed[rows:]], axis=1)


def attention_first_kernel(queries_ref, kv_ref, *state_refs):
    core = lax.axis_index("core")
    for i in range(2):
        for ref, value in zip(state_refs, attend(queries_ref[i], kv_ref, core, None)):
            ref[i] = jnp.broadcast_to(value, ref.shape[1:])


def attention_second_kernel(queries_ref, kv_ref, top_ref, total_ref, summed_ref, out_ref):
    core = lax.axis_index("core")
    heads = []
    for i in range(2):
        state = top_ref[i, :, :1], total_ref[i, :, :1], summed_ref[i]
        heads.append(finish(attend(queries_ref[i], kv_ref, 1 - core, state)))
    first = lax.axis_index("xh") == 0
    heads = [jnp.where(first, heads[0], heads[1]), jnp.where(first, heads[1], heads[0])]
    for i in range(N_Z):
        out_ref[i] = heads[i % 2]


def project(mask_ref, heads_ref, weight_ref, of_pair, of_sibling):
    columns = weight_ref.shape[1]
    parity, core = lax.rem(lax.axis_index("z"), 2), lax.axis_index("core")
    from_chip = 1 - parity if of_pair else parity
    from_core = 1 - core if of_sibling else core
    total = jnp.zeros((heads_ref.shape[1], columns), jnp.float32)
    for z in range(N_Z):
        rows = []
        for i in range(2):
            block = ((z * 2 + from_chip) * 2 + from_core) * 2 + i
            at = pl.ds(pl.multiple_of(block * BLOCK, BLOCK), BLOCK)
            line = []
            for j in range(columns // BLOCK):
                keep = mask_ref[j, block].astype(jnp.float32).astype(jnp.bfloat16)
                line.append(weight_ref[at, j * BLOCK : (j + 1) * BLOCK] * keep)
            rows.append(jnp.concatenate(line, axis=1))
        pruned = jnp.concatenate(rows, axis=0)
        total += jnp.dot(heads_ref[z], pruned, preferred_element_type=jnp.float32)
    return total


def project_first_kernel(mask_ref, weight_ref, self_ref, out_ref):
    out_ref[...] = project(mask_ref, self_ref, weight_ref, False, False)


def project_second_kernel(mask_ref, weight_ref, sibling_ref, pair_ref, part_ref, out_ref):
    part = part_ref[...] + project(mask_ref, sibling_ref, weight_ref, False, True)
    out_ref[...] = part + project(mask_ref, pair_ref, weight_ref, True, False)


def project_third_kernel(mask_ref, weight_ref, sibling_ref, part_ref, out_ref):
    part = part_ref[...] + project(mask_ref, sibling_ref, weight_ref, True, True)
    out_ref[...] = part.astype(out_ref.dtype)


def per_device(queries, keys, values, out_weight, block_mask):
    rows = queries.shape[0]
    columns = out_weight.shape[1]
    part = rows // (2 * N_SQUARE)
    mask = block_mask.T
    params = pltpu.CompilerParams(vmem_limit_bytes=32 * 2**20)
    shape = jax.ShapeDtypeStruct
    cost = pl.CostEstimate(flops=2**29, bytes_accessed=2**21, transcendentals=2**20)
    swap = [(0, 1), (1, 0)]
    partner_queries = lax.ppermute(queries, "xh", swap)
    spread = pl.pallas_call(
        spread_kernel,
        out_shape=shape((N_SEQ, part, 2 * HD), jnp.bfloat16),
        in_specs=[ANY] * 2,
        out_specs=VMEM,
        scratch_shapes=[pltpu.VMEM((rows, 2 * HD), jnp.bfloat16), pltpu.SemaphoreType.DMA((2,))],
        name="spread_kv",
    )(keys, values)
    piece = lax.all_to_all(spread, SEQ, 0, 0, tiled=True)
    stacked = pl.pallas_call(
        stack_kernel,
        out_shape=shape((2, 2 * rows, HD), jnp.bfloat16),
        in_specs=[VMEM] * 2,
        out_specs=VMEM,
        compiler_params=params,
        cost_estimate=pl.CostEstimate(flops=2**36, bytes_accessed=2**18, transcendentals=0),
        name="stack_queries",
    )(queries, partner_queries)
    piece, stacked = lax.optimization_barrier((piece, stacked))
    square = pl.pallas_call(
        square_kernel,
        out_shape=shape((N_SQUARE, N_SEQ, part, 2 * HD), jnp.bfloat16),
        in_specs=[VMEM],
        out_specs=VMEM,
        compiler_params=params,
        name="square",
    )(piece)
    own = lax.all_to_all(square, PLANE, 0, 0, axis_index_groups=square_groups(), tiled=True)
    other = lax.ppermute(own, "core", swap)
    state = pl.pallas_call(
        attention_first_kernel,
        out_shape=[shape((2, 2 * rows, HD), jnp.float32)] * 3,
        in_specs=[VMEM] * 2,
        out_specs=[VMEM] * 3,
        compiler_params=params,
        cost_estimate=cost,
        name="attention_first",
    )(stacked, own)
    heads = pl.pallas_call(
        attention_second_kernel,
        out_shape=shape((N_Z, rows, 2 * HD), jnp.bfloat16),
        in_specs=[VMEM] * 5,
        out_specs=VMEM,
        compiler_params=params,
        cost_estimate=cost,
        name="attention_second",
    )(stacked, other, *state)
    along_z = lax.all_to_all(heads, "z", 0, 0, tiled=True)
    from_pair = lax.ppermute(along_z, RING, z_pairs())
    sibling = lax.ppermute(along_z, "core", swap)
    pair_sibling = lax.ppermute(from_pair, "core", swap)

    def call(kernel, name, dtype, *arrays):
        return pl.pallas_call(
            kernel,
            out_shape=shape((rows, columns), dtype),
            in_specs=[SMEM] + [VMEM] * (1 + len(arrays)),
            out_specs=VMEM,
            compiler_params=params,
            cost_estimate=pl.CostEstimate(flops=2**27, bytes_accessed=2**21, transcendentals=0),
            name=name,
        )(mask, out_weight, *arrays)

    first = call(project_first_kernel, "project_first", jnp.float32, along_z)
    second = call(project_second_kernel, "project_second", jnp.float32, sibling, from_pair, first)
    return call(project_third_kernel, "project_third", jnp.bfloat16, pair_sibling, second)


def solution(mesh):
    fine = Mesh(mesh.devices.reshape(SIZES), AXES)
    return jax.shard_map(
        per_device,
        mesh=fine,
        in_specs=(P(SEQ, FSDP), P(SEQ, None), P(SEQ, None), P(None, FSDP), P(None, FSDP)),
        out_specs=P(SEQ, FSDP),
        check_vma=False,
    )
```

```python
import functools
import math

import jax
import jax.numpy as jnp
from jax import lax
from jax.experimental import pallas as pl
from jax.experimental.pallas import tpu as pltpu
from jax.sharding import Mesh
from jax.sharding import PartitionSpec as P

HD = 128
BLOCK = 128
SIZES = (4, 2, 2, 2, 8, 2, 2)
AXES = ("y", "yp", "xl", "xp", "z", "xh", "core")
SEQ = ("y", "yp", "xl", "xp")
N_SQUARE = 4
PLANE = ("y", "yp", "xl", "xp", "xh", "core")
RING = ("z", "core")
FSDP = ("z", "xh", "core")
N_SEQ = 32
N_Z = 8
FACTOR = math.log2(math.e) / math.sqrt(HD)
LOWEST = -1e30
CHUNK = 256
ANY = pl.BlockSpec(memory_space=pl.ANY)
VMEM = pl.BlockSpec(memory_space=pltpu.VMEM)
SMEM = pl.BlockSpec(memory_space=pltpu.SMEM)


def square_groups():
    groups = []
    for core in range(2):
        for top in range(core, 8, 2):
            for left in range(core, 8, 2):
                group = [None] * N_SQUARE
                for y in (top, (top + 1) % 8):
                    for x in (left, (left + 1) % 8):
                        flat = (y * 4 + x % 4) * 2 + x // 4
                        group[y % 2 * 2 + x % 2] = flat * 2 + core
                groups.append(group)
    return groups


def z_pairs():
    pairs = []
    for z in range(8):
        for core in range(2):
            other = z ^ 1 if core == 0 else (((z + 1) ^ 1) - 1) % 8
            pairs.append((z * 2 + core, other * 2 + core))
    return pairs


def spread_kernel(keys_ref, values_ref, out_ref, block, sems):
    part = out_ref.shape[1]
    column = pl.multiple_of(lax.axis_index("z") * HD, HD)
    core = lax.axis_index("core")
    copies = [
        pltpu.make_async_copy(
            source.at[:, pl.ds(column, HD)], block.at[:, i * HD : (i + 1) * HD], sems.at[i]
        )
        for i, source in enumerate((keys_ref, values_ref))
    ]
    for copy in copies:
        copy.start()
    for copy in copies:
        copy.wait()
    pieces = [
        block[pl.ds(pl.multiple_of((place * 2 + core) * part, part), part), :]
        for place in range(N_SQUARE)
    ]
    for i in range(N_SEQ):
        out_ref[i] = pieces[i // 4 % 2 * 2 + i % 2]


def square_kernel(piece_ref, out_ref):
    for i in range(N_SQUARE):
        out_ref[i] = piece_ref[...]


def attend(queries_ref, kv_ref, from_core, state):
    rows = queries_ref.shape[0]
    part = kv_ref.shape[2]
    width = N_SQUARE * N_SEQ * part
    seq = lax.axis_index("y") * 8 + lax.axis_index("yp") * 4 + lax.axis_index("xl") * 2
    start = (seq + lax.axis_index("xp")) * rows
    q = jnp.concatenate([queries_ref[:, :HD], queries_ref[:, HD:]], axis=0)
    query_pos = start + lax.broadcasted_iota(jnp.int32, (2 * rows, 1), 0) % rows
    chunks = []
    for first in range(0, width, CHUNK):
        place, entry = divmod(first // part, N_SEQ)
        entries = kv_ref[place, entry : entry + CHUNK // part]
        column = first + lax.broadcasted_iota(jnp.int32, (1, CHUNK), 1)
        block = column // part
        token = (place * 2 + from_core) * part + column % part
        key_pos = block % N_SEQ * rows + token
        key = entries[:, :, :HD].reshape(CHUNK, HD)
        score = lax.dot_general(q, key, (((1,), (1,)), ((), ())), preferred_element_type=jnp.float32)
        score = jnp.where(query_pos >= key_pos, score, jnp.float32(LOWEST))
        chunks.append((score, entries[:, :, HD:].reshape(CHUNK, HD)))
    tops = [jnp.max(score, axis=1, keepdims=True) for score, _ in chunks]
    top = functools.reduce(jnp.maximum, tops if state is None else tops + [state[0]])
    total = summed = 0.0
    for score, value in chunks:
        expo = jnp.exp2((score - top) * FACTOR)
        total = total + jnp.sum(expo, axis=1, keepdims=True)
        summed = summed + jnp.dot(
            expo.astype(jnp.bfloat16), value, preferred_element_type=jnp.float32
        )
    if state is not None:
        fix = jnp.exp2((state[0] - top) * FACTOR)
        total = total + state[1] * fix
        summed = summed + state[2] * fix
    return top, total, summed


def finish(state):
    _, total, summed = state
    rows = total.shape[0] // 2
    normed = (summed / total).astype(jnp.bfloat16)
    return jnp.concatenate([normed[:rows], normed[rows:]], axis=1)


def attention_first_kernel(queries_ref, partner_ref, kv_ref, *state_refs):
    core = lax.axis_index("core")
    for i, queries in enumerate((queries_ref, partner_ref)):
        for ref, value in zip(state_refs, attend(queries, kv_ref, core, None)):
            ref[i] = jnp.broadcast_to(value, ref.shape[1:])


def attention_second_kernel(queries_ref, partner_ref, kv_ref, top_ref, total_ref, summed_ref, out_ref):
    core = lax.axis_index("core")
    heads = []
    for i, queries in enumerate((queries_ref, partner_ref)):
        state = top_ref[i, :, :1], total_ref[i, :, :1], summed_ref[i]
        heads.append(finish(attend(queries, kv_ref, 1 - core, state)))
    first = lax.axis_index("xh") == 0
    heads = [jnp.where(first, heads[0], heads[1]), jnp.where(first, heads[1], heads[0])]
    for i in range(N_Z):
        out_ref[i] = heads[i % 2]


def project(mask_ref, heads_ref, weight_ref, of_pair, of_sibling):
    columns = weight_ref.shape[1]
    parity, core = lax.rem(lax.axis_index("z"), 2), lax.axis_index("core")
    from_chip = 1 - parity if of_pair else parity
    from_core = 1 - core if of_sibling else core
    total = jnp.zeros((heads_ref.shape[1], columns), jnp.float32)
    for z in range(N_Z):
        rows = []
        for i in range(2):
            block = ((z * 2 + from_chip) * 2 + from_core) * 2 + i
            at = pl.ds(pl.multiple_of(block * BLOCK, BLOCK), BLOCK)
            line = []
            for j in range(columns // BLOCK):
                keep = mask_ref[j, block].astype(jnp.float32).astype(jnp.bfloat16)
                line.append(weight_ref[at, j * BLOCK : (j + 1) * BLOCK] * keep)
            rows.append(jnp.concatenate(line, axis=1))
        pruned = jnp.concatenate(rows, axis=0)
        total += jnp.dot(heads_ref[z], pruned, preferred_element_type=jnp.float32)
    return total


def project_first_kernel(mask_ref, weight_ref, self_ref, out_ref):
    out_ref[...] = project(mask_ref, self_ref, weight_ref, False, False)


def project_second_kernel(mask_ref, weight_ref, sibling_ref, pair_ref, part_ref, out_ref):
    part = part_ref[...] + project(mask_ref, sibling_ref, weight_ref, False, True)
    out_ref[...] = part + project(mask_ref, pair_ref, weight_ref, True, False)


def project_third_kernel(mask_ref, weight_ref, sibling_ref, part_ref, out_ref):
    part = part_ref[...] + project(mask_ref, sibling_ref, weight_ref, True, True)
    out_ref[...] = part.astype(out_ref.dtype)


def per_device(queries, keys, values, out_weight, block_mask):
    rows = queries.shape[0]
    columns = out_weight.shape[1]
    part = rows // (2 * N_SQUARE)
    mask = block_mask.T
    params = pltpu.CompilerParams(vmem_limit_bytes=32 * 2**20)
    shape = jax.ShapeDtypeStruct
    cost = pl.CostEstimate(flops=2**29, bytes_accessed=2**21, transcendentals=2**20)
    swap = [(0, 1), (1, 0)]
    partner_queries = lax.ppermute(queries, "xh", swap)
    spread = pl.pallas_call(
        spread_kernel,
        out_shape=shape((N_SEQ, part, 2 * HD), jnp.bfloat16),
        in_specs=[ANY] * 2,
        out_specs=VMEM,
        scratch_shapes=[pltpu.VMEM((rows, 2 * HD), jnp.bfloat16), pltpu.SemaphoreType.DMA((2,))],
        name="spread_kv",
    )(keys, values)
    piece = lax.all_to_all(spread, SEQ, 0, 0, tiled=True)
    piece, partner_queries = lax.optimization_barrier((piece, partner_queries))
    square = pl.pallas_call(
        square_kernel,
        out_shape=shape((N_SQUARE, N_SEQ, part, 2 * HD), jnp.bfloat16),
        in_specs=[VMEM],
        out_specs=VMEM,
        compiler_params=params,
        name="square",
    )(piece)
    own = lax.all_to_all(square, PLANE, 0, 0, axis_index_groups=square_groups(), tiled=True)
    other = lax.ppermute(own, "core", swap)
    state = pl.pallas_call(
        attention_first_kernel,
        out_shape=[shape((2, 2 * rows, HD), jnp.float32)] * 3,
        in_specs=[VMEM] * 3,
        out_specs=[VMEM] * 3,
        compiler_params=params,
        cost_estimate=cost,
        name="attention_first",
    )(queries, partner_queries, own)
    heads = pl.pallas_call(
        attention_second_kernel,
        out_shape=shape((N_Z, rows, 2 * HD), jnp.bfloat16),
        in_specs=[VMEM] * 6,
        out_specs=VMEM,
        compiler_params=params,
        cost_estimate=cost,
        name="attention_second",
    )(queries, partner_queries, other, *state)
    along_z = lax.all_to_all(heads, "z", 0, 0, tiled=True)
    from_pair = lax.ppermute(along_z, RING, z_pairs())
    sibling = lax.ppermute(along_z, "core", swap)

    def call(kernel, name, dtype, *arrays):
        return pl.pallas_call(
            kernel,
            out_shape=shape((rows, columns), dtype),
            in_specs=[SMEM] + [VMEM] * (1 + len(arrays)),
            out_specs=VMEM,
            compiler_params=params,
            cost_estimate=pl.CostEstimate(flops=2**27, bytes_accessed=2**21, transcendentals=0),
            name=name,
        )(mask, out_weight, *arrays)

    first = call(project_first_kernel, "project_first", jnp.float32, along_z)
    from_pair, first = lax.optimization_barrier((from_pair, first))
    pair_sibling = lax.ppermute(from_pair, "core", swap)
    second = call(project_second_kernel, "project_second", jnp.float32, sibling, from_pair, first)
    return call(project_third_kernel, "project_third", jnp.bfloat16, pair_sibling, second)


def solution(mesh):
    fine = Mesh(mesh.devices.reshape(SIZES), AXES)
    return jax.shard_map(
        per_device,
        mesh=fine,
        in_specs=(P(SEQ, FSDP), P(SEQ, None), P(SEQ, None), P(None, FSDP), P(None, FSDP)),
        out_specs=P(SEQ, FSDP),
        check_vma=False,
    )
```

```python
import functools
import math

import jax
import jax.numpy as jnp
from jax import lax
from jax.experimental import pallas as pl
from jax.experimental.pallas import tpu as pltpu
from jax.sharding import Mesh
from jax.sharding import PartitionSpec as P

HD = 128
BLOCK = 128
SIZES = (4, 2, 2, 2, 8, 2, 2)
AXES = ("y", "yp", "xl", "xp", "z", "xh", "core")
SEQ = ("y", "yp", "xl", "xp")
N_SQUARE = 4
PLANE = ("y", "yp", "xl", "xp", "xh", "core")
RING = ("z", "core")
FSDP = ("z", "xh", "core")
N_SEQ = 32
N_Z = 8
FACTOR = math.log2(math.e) / math.sqrt(HD)
LOWEST = -1e30
CHUNK = 256
ANY = pl.BlockSpec(memory_space=pl.ANY)
VMEM = pl.BlockSpec(memory_space=pltpu.VMEM)
SMEM = pl.BlockSpec(memory_space=pltpu.SMEM)


def square_groups():
    groups = []
    for core in range(2):
        for top in range(core, 8, 2):
            for left in range(core, 8, 2):
                group = [None] * N_SQUARE
                for y in (top, (top + 1) % 8):
                    for x in (left, (left + 1) % 8):
                        flat = (y * 4 + x % 4) * 2 + x // 4
                        group[y % 2 * 2 + x % 2] = flat * 2 + core
                groups.append(group)
    return groups


def z_pairs():
    pairs = []
    for z in range(8):
        for core in range(2):
            other = z ^ 1 if core == 0 else (((z + 1) ^ 1) - 1) % 8
            pairs.append((z * 2 + core, other * 2 + core))
    return pairs


def spread_kernel(keys_ref, values_ref, out_ref, block, sems):
    part = out_ref.shape[1]
    column = pl.multiple_of(lax.axis_index("z") * HD, HD)
    core = lax.axis_index("core")
    copies = [
        pltpu.make_async_copy(
            source.at[:, pl.ds(column, HD)], block.at[:, i * HD : (i + 1) * HD], sems.at[i]
        )
        for i, source in enumerate((keys_ref, values_ref))
    ]
    for copy in copies:
        copy.start()
    for copy in copies:
        copy.wait()
    pieces = [
        block[pl.ds(pl.multiple_of((place * 2 + core) * part, part), part), :]
        for place in range(N_SQUARE)
    ]
    for i in range(N_SEQ):
        out_ref[i] = pieces[i // 4 % 2 * 2 + i % 2]


def square_kernel(piece_ref, out_ref):
    for i in range(N_SQUARE):
        out_ref[i] = piece_ref[...]


def attend(queries_ref, kv_ref, from_core, state):
    rows = queries_ref.shape[0]
    part = kv_ref.shape[2]
    width = N_SQUARE * N_SEQ * part
    seq = lax.axis_index("y") * 8 + lax.axis_index("yp") * 4 + lax.axis_index("xl") * 2
    start = (seq + lax.axis_index("xp")) * rows
    q = jnp.concatenate([queries_ref[:, :HD], queries_ref[:, HD:]], axis=0)
    query_pos = start + lax.broadcasted_iota(jnp.int32, (2 * rows, 1), 0) % rows
    chunks = []
    for first in range(0, width, CHUNK):
        place, entry = divmod(first // part, N_SEQ)
        entries = kv_ref[place, entry : entry + CHUNK // part]
        column = first + lax.broadcasted_iota(jnp.int32, (1, CHUNK), 1)
        block = column // part
        token = (place * 2 + from_core) * part + column % part
        key_pos = block % N_SEQ * rows + token
        key = entries[:, :, :HD].reshape(CHUNK, HD)
        score = lax.dot_general(q, key, (((1,), (1,)), ((), ())), preferred_element_type=jnp.float32)
        score = jnp.where(query_pos >= key_pos, score, jnp.float32(LOWEST))
        chunks.append((score, entries[:, :, HD:].reshape(CHUNK, HD)))
    tops = [jnp.max(score, axis=1, keepdims=True) for score, _ in chunks]
    top = functools.reduce(jnp.maximum, tops if state is None else tops + [state[0]])
    total = summed = 0.0
    for score, value in chunks:
        expo = jnp.exp2((score - top) * FACTOR)
        total = total + jnp.sum(expo, axis=1, keepdims=True)
        summed = summed + jnp.dot(
            expo.astype(jnp.bfloat16), value, preferred_element_type=jnp.float32
        )
    if state is not None:
        fix = jnp.exp2((state[0] - top) * FACTOR)
        total = total + state[1] * fix
        summed = summed + state[2] * fix
    return top, total, summed


def finish(state):
    _, total, summed = state
    rows = total.shape[0] // 2
    normed = (summed / total).astype(jnp.bfloat16)
    return jnp.concatenate([normed[:rows], normed[rows:]], axis=1)


def attention_first_kernel(queries_ref, partner_ref, kv_ref, *state_refs):
    core = lax.axis_index("core")
    for i, queries in enumerate((queries_ref, partner_ref)):
        for ref, value in zip(state_refs, attend(queries, kv_ref, core, None)):
            ref[i] = jnp.broadcast_to(value, ref.shape[1:])


def attention_second_kernel(queries_ref, partner_ref, kv_ref, top_ref, total_ref, summed_ref, out_ref):
    core = lax.axis_index("core")
    heads = []
    for i, queries in enumerate((queries_ref, partner_ref)):
        state = top_ref[i, :, :1], total_ref[i, :, :1], summed_ref[i]
        heads.append(finish(attend(queries, kv_ref, 1 - core, state)))
    first = lax.axis_index("xh") == 0
    heads = [jnp.where(first, heads[0], heads[1]), jnp.where(first, heads[1], heads[0])]
    for i in range(N_Z):
        out_ref[i] = heads[i % 2]


def prune_kernel(mask_ref, weight_ref, out_ref):
    rows, columns = weight_ref.shape
    for block in range(rows // BLOCK):
        for j in range(columns // BLOCK):
            at = slice(block * BLOCK, (block + 1) * BLOCK), slice(j * BLOCK, (j + 1) * BLOCK)
            keep = mask_ref[j, block].astype(jnp.float32).astype(jnp.bfloat16)
            out_ref[at] = weight_ref[at] * keep


def project(heads_ref, weight_ref, of_pair, of_sibling):
    parity, core = lax.rem(lax.axis_index("z"), 2), lax.axis_index("core")
    from_chip = 1 - parity if of_pair else parity
    from_core = 1 - core if of_sibling else core
    width = heads_ref.shape[2]
    total = jnp.zeros((heads_ref.shape[1], weight_ref.shape[1]), jnp.float32)
    for z in range(N_Z):
        part = (z * 2 + from_chip) * 2 + from_core
        rows = weight_ref[pl.ds(pl.multiple_of(part * width, width), width), :]
        total += jnp.dot(heads_ref[z], rows, preferred_element_type=jnp.float32)
    return total


def project_first_kernel(weight_ref, self_ref, out_ref):
    out_ref[...] = project(self_ref, weight_ref, False, False)


def project_second_kernel(weight_ref, sibling_ref, pair_ref, part_ref, out_ref):
    part = part_ref[...] + project(sibling_ref, weight_ref, False, True)
    out_ref[...] = part + project(pair_ref, weight_ref, True, False)


def project_third_kernel(weight_ref, sibling_ref, part_ref, out_ref):
    part = part_ref[...] + project(sibling_ref, weight_ref, True, True)
    out_ref[...] = part.astype(out_ref.dtype)


def per_device(queries, keys, values, out_weight, block_mask):
    rows = queries.shape[0]
    columns = out_weight.shape[1]
    part = rows // (2 * N_SQUARE)
    mask = block_mask.T
    params = pltpu.CompilerParams(vmem_limit_bytes=32 * 2**20)
    shape = jax.ShapeDtypeStruct
    cost = pl.CostEstimate(flops=2**29, bytes_accessed=2**21, transcendentals=2**20)
    swap = [(0, 1), (1, 0)]
    partner_queries = lax.ppermute(queries, "xh", swap)
    spread = pl.pallas_call(
        spread_kernel,
        out_shape=shape((N_SEQ, part, 2 * HD), jnp.bfloat16),
        in_specs=[ANY] * 2,
        out_specs=VMEM,
        scratch_shapes=[pltpu.VMEM((rows, 2 * HD), jnp.bfloat16), pltpu.SemaphoreType.DMA((2,))],
        name="spread_kv",
    )(keys, values)
    piece = lax.all_to_all(spread, SEQ, 0, 0, tiled=True)
    piece, partner_queries = lax.optimization_barrier((piece, partner_queries))
    square = pl.pallas_call(
        square_kernel,
        out_shape=shape((N_SQUARE, N_SEQ, part, 2 * HD), jnp.bfloat16),
        in_specs=[VMEM],
        out_specs=VMEM,
        compiler_params=params,
        name="square",
    )(piece)
    own = lax.all_to_all(square, PLANE, 0, 0, axis_index_groups=square_groups(), tiled=True)
    other = lax.ppermute(own, "core", swap)
    state = pl.pallas_call(
        attention_first_kernel,
        out_shape=[shape((2, 2 * rows, HD), jnp.float32)] * 3,
        in_specs=[VMEM] * 3,
        out_specs=[VMEM] * 3,
        compiler_params=params,
        cost_estimate=cost,
        name="attention_first",
    )(queries, partner_queries, own)
    heads = pl.pallas_call(
        attention_second_kernel,
        out_shape=shape((N_Z, rows, 2 * HD), jnp.bfloat16),
        in_specs=[VMEM] * 6,
        out_specs=VMEM,
        compiler_params=params,
        cost_estimate=cost,
        name="attention_second",
    )(queries, partner_queries, other, *state)
    heads, mask = lax.optimization_barrier((heads, mask))
    pruned = pl.pallas_call(
        prune_kernel,
        out_shape=shape(out_weight.shape, jnp.bfloat16),
        in_specs=[SMEM, VMEM],
        out_specs=VMEM,
        compiler_params=params,
        cost_estimate=pl.CostEstimate(flops=2**30, bytes_accessed=2**23, transcendentals=0),
        name="prune",
    )(mask, out_weight)
    along_z = lax.all_to_all(heads, "z", 0, 0, tiled=True)
    along_z, pruned = lax.optimization_barrier((along_z, pruned))
    from_pair = lax.ppermute(along_z, RING, z_pairs())
    sibling = lax.ppermute(along_z, "core", swap)

    def call(kernel, name, dtype, *arrays):
        return pl.pallas_call(
            kernel,
            out_shape=shape((rows, columns), dtype),
            in_specs=[VMEM] * (1 + len(arrays)),
            out_specs=VMEM,
            compiler_params=params,
            cost_estimate=pl.CostEstimate(flops=2**27, bytes_accessed=2**21, transcendentals=0),
            name=name,
        )(pruned, *arrays)

    first = call(project_first_kernel, "project_first", jnp.float32, along_z)
    from_pair, first = lax.optimization_barrier((from_pair, first))
    pair_sibling = lax.ppermute(from_pair, "core", swap)
    second = call(project_second_kernel, "project_second", jnp.float32, sibling, from_pair, first)
    return call(project_third_kernel, "project_third", jnp.bfloat16, pair_sibling, second)


def solution(mesh):
    fine = Mesh(mesh.devices.reshape(SIZES), AXES)
    return jax.shard_map(
        per_device,
        mesh=fine,
        in_specs=(P(SEQ, FSDP), P(SEQ, None), P(SEQ, None), P(None, FSDP), P(None, FSDP)),
        out_specs=P(SEQ, FSDP),
        check_vma=False,
    )
```
